256 devices in a mesh: lat: 32 (over y, z_hi, core), lon: 8 (over z_lo, x).
Axes of the slice: x: 4, y: 4, z: 8 (z_hi: 4, z_lo: 2; z = z_hi * 2 + z_lo), core: 2. Of those that a mesh axis runs over, the one named last changes fastest.
Arguments:
- grid: bfloat16 [16, 5120, 11264], P(None, 'lat', 'lon'), may hold values from -6 to 6
- cycle_points: int32 [5120], replicated, may hold values from 20 to 10256, as said below
- pair_slot: int32 [160], replicated, may hold values from 0 to 159, each once
- polys: bfloat16 [160, 321, 2560], P('lat'), may hold values from -6 to 6
Outputs:
- spectra: float32 [16, 160, 321, 2], P('lon', 'lat')
The draws below stay inside these ranges and needn't reach their ends.
Inputs may be any that keep to these rules, and one draw needn't show every extreme that they name: cycle_points[l] equals cycle_points[5119 - l], is a multiple of 4 and is at least 20 + 4 * min(l, 5119 - l); the largest value is reached at the equator. `pair_slot`: each slot number appears once.
All inputs are finite; a program needn't handle non-finite values.
Results may differ from the reference program's by a relative error of at most 0.0023.
Values may be sent and summed in bfloat16 or wider, within the bound.
A program may use at most 192 MiB of HBM per device.

```python
import math
import jax
import jax.numpy as jnp
from jax import lax

NLAT = 5120
FIELDS = 16
MW = 320
BLK = 128
NH = 2560
M0 = 2240
ROW = 11264
PAIRS = 160
ROWS = 321


def draw_cycle_points(key, part):
    key = jax.random.fold_in(key, 11)
    hemisphere = NLAT // 2
    jitter_steps = jax.random.randint(key, (hemisphere,), 0, 9, dtype=jnp.int32)
    latitude = jnp.arange(NLAT, dtype=jnp.int32)
    from_pole = jnp.minimum(latitude, NLAT - 1 - latitude)
    counts = 20 + 4 * (from_pole + jitter_steps[from_pole])
    return jnp.minimum(counts, 20 + 4 * (hemisphere - 1)).astype(jnp.int32)


def block_scale(rng, dims, shards, low, top_value):
    def one(dim, shards_of):
        heights = jax.random.uniform(jax.random.fold_in(jax.random.fold_in(rng, 6), dim), (shards_of,), jnp.float32, low / len(shards), top_value / len(shards))
        return jnp.repeat(jnp.exp(heights), dims[dim] // shards_of).reshape((-1,) + (1,) * (len(dims) - dim - 1))

    gain = one(*shards[0])
    for cut in shards[1:]:
        gain = gain * one(*cut)
    return gain


def centred(stream_key, shape, width, reach, shards=(), kind=jnp.bfloat16):
    factor_of = block_scale(stream_key, shape, shards, -0.22, 0.18) if shards else 1.0
    drawn = jax.random.normal(stream_key, shape, jnp.float32) * width * factor_of
    return jnp.minimum(jnp.maximum(drawn, -reach), reach).astype(kind)


def setup_inputs(seed: int = 0) -> dict:
    splits = jax.random.split(jax.random.key(seed), 5)
    grid = centred(splits[0], (FIELDS, NLAT, ROW), 1.0, 6.0, ((1, 32), (2, 8)))
    cycle_points = draw_cycle_points(jax.random.fold_in(splits[4], 71), 0)
    pair_slot = jax.random.permutation(splits[2], PAIRS).astype(jnp.int32)
    polys = centred(splits[3], (PAIRS, ROWS, NH), 1.0, 6.0, ((0, 32),))
    return {"grid": grid, "cycle_points": cycle_points, "pair_slot": pair_slot, "polys": polys}


two_pi = 2.0 * math.pi


def phase_angle(index_table, counts_cube):
    return two_pi * index_table.astype(jnp.float32) / counts_cube.astype(jnp.float32)


def cycle_transform(values, cycle_counts, wave_numbers, first_block):
    block_width = values.shape[3]
    window = wave_numbers.shape[0]
    highest = lax.Precision.HIGHEST
    offsets = jnp.arange(block_width, dtype=jnp.int32)
    blocks = first_block + jnp.arange(values.shape[2], dtype=jnp.int32)
    counts_cube = cycle_counts[:, None, None]
    inner_index = (wave_numbers[None, None, :] * offsets[None, :, None]) % counts_cube
    inner_angle = phase_angle(inner_index, counts_cube)
    inner_table = jnp.concatenate([jnp.cos(inner_angle), jnp.sin(inner_angle)], axis=-1).astype(jnp.bfloat16)
    positions = blocks[:, None] * block_width + offsets[None, :]
    inside = positions[None, :, :] < counts_cube
    masked = jnp.where(inside[None], values, jnp.zeros_like(values))
    partial_sums = jnp.einsum("frab,rbc->frac", masked.astype(jnp.float32), inner_table.astype(jnp.float32), precision=highest)
    cos_sums = partial_sums[..., :window]
    sin_sums = partial_sums[..., window:]
    outer_index = (wave_numbers[None, None, :] * (block_width * blocks)[None, :, None]) % counts_cube
    outer_angle = phase_angle(outer_index, counts_cube)
    outer_cos = jnp.cos(outer_angle)
    outer_sin = jnp.sin(outer_angle)
    real_part = jnp.einsum("rak,frak->fkr", outer_cos, cos_sums, precision=highest) - jnp.einsum("rak,frak->fkr", outer_sin, sin_sums, precision=highest)
    imag_part = -(jnp.einsum("rak,frak->fkr", outer_sin, cos_sums, precision=highest) + jnp.einsum("rak,frak->fkr", outer_cos, sin_sums, precision=highest))
    resolved = 2 * wave_numbers[:, None] < cycle_counts[None, :]
    row_scale = jnp.where(resolved, 1.0 / cycle_counts[None, :].astype(jnp.float32), 0.0).astype(jnp.float32)
    return jnp.stack([real_part * row_scale, imag_part * row_scale], axis=2)


def select_rows(first_out, second_out, pair_index):
    row_index = jnp.arange(ROWS, dtype=jnp.int32)
    split_row = MW - pair_index
    in_first = row_index < split_row
    degree = jnp.where(in_first, row_index, row_index - split_row)
    even_rows = degree % 2 == 0

    def parity(products):
        return jnp.where(even_rows[:, None, None], products[:, 0], products[:, 1])

    return jnp.where(in_first[:, None, None], parity(first_out), parity(second_out))


def reference(grid, cycle_points, pair_slot, polys):
    field_count = grid.shape[0]
    cycle_block = 64 if NLAT % 64 == 0 else NLAT
    block_count = NLAT // cycle_block
    wave_numbers = M0 + jnp.arange(MW, dtype=jnp.int32)
    values = grid.reshape(field_count, block_count, cycle_block, ROW // BLK, BLK)
    values = jnp.moveaxis(values, 1, 0)
    counts = cycle_points.reshape(block_count, cycle_block)

    def one_block(pieces):
        return cycle_transform(pieces[0], pieces[1], wave_numbers, 0)

    fourier = lax.map(one_block, (values, counts))
    fourier = jnp.moveaxis(fourier, 0, 3).reshape(field_count, MW, 2, NLAT)
    north_rows = fourier[..., :NH]
    south_rows = jnp.flip(fourier[..., NH:], axis=-1)
    folded = jnp.stack([north_rows + south_rows, north_rows - south_rows])

    def one_slot(pieces):
        poly_block, pair_index = pieces
        first_wave = lax.dynamic_index_in_dim(folded, pair_index, axis=2, keepdims=False)
        second_wave = lax.dynamic_index_in_dim(folded, MW - 1 - pair_index, axis=2, keepdims=False)
        weights = poly_block.astype(jnp.float32)
        first_out = jnp.einsum("rh,afqh->rafq", weights, first_wave, precision=lax.Precision.HIGHEST)
        second_out = jnp.einsum("rh,afqh->rafq", weights, second_wave, precision=lax.Precision.HIGHEST)
        return select_rows(first_out, second_out, pair_index)

    spectra = lax.map(one_slot, (polys, pair_slot))
    return jnp.transpose(spectra, (2, 0, 1, 3))
```

```python
import functools, math
import jax, jax.numpy as jnp
from jax import lax
from jax.experimental import pallas as pl
from jax.experimental.pallas import tpu as pltpu
from jax.sharding import PartitionSpec as P

MW = 320
M0 = 2240
ROWS = 321

LB = 16

def sincos_turn(u):
    w = u - jnp.floor(u + 0.5)
    x = w * math.pi
    y = x * x
    s = x * (1.0 + y * (-1/6 + y * (1/120 + y * (-1/5040 + y * (1/362880 + y * (-1/39916800 + y * (1/6227020800)))))))
    c = 1.0 + y * (-1/2 + y * (1/24 + y * (-1/720 + y * (1/40320 + y * (-1/3628800 + y * (1/479001600))))))
    return 1.0 - 2.0 * s * s, 2.0 * s * c

def fmod(x, c):
    q = jnp.floor(x / c)
    r = x - q * c
    r = jnp.where(r < 0, r + c, r)
    return jnp.where(r >= c, r - c, r)

def cmul(p, q):
    return (p[0] * q[0] - p[1] * q[1], p[0] * q[1] + p[1] * q[0])

def kernel(meta, cnt, ccol, mrow, grid, out, gf, SE, R2, OC, OS, WC, WS, ob):
    i = pl.program_id(0)
    first = meta[0]
    lane = lax.broadcasted_iota(jnp.int32, (8, 128), 1)
    cosl = (lane % 4) < 2
    for g in range(2):
        c = ccol[pl.ds(pl.multiple_of(i * LB + g * 8, 8), 8), :]
        for kt in range(3):
            m = jnp.broadcast_to(mrow[0:1, kt * 128:(kt + 1) * 128], (8, 128))
            r1 = fmod(m, c)
            e1 = sincos_turn(r1 / c)
            rp = fmod(r1 * 128.0, c)
            p1 = sincos_turn(rp / c)
            r0 = fmod(rp * (first // 128 + 5).astype(jnp.float32), c)
            w = sincos_turn(r0 / c)
            scale = jnp.where(2.0 * m < c, 1.0 / c, 0.0)
            WC[g, kt] = w[0] * scale
            if kt == 2:
                WS[g, kt] = jnp.where(cosl, w[1] * scale, -(w[1] * scale))
            else:
                WS[g, kt] = w[1] * scale
            pj = p1
            for j in range(1, 6):
                if j > 1:
                    pj = cmul(pj, p1)
                OC[g, kt, j - 1] = pj[0]
                OS[g, kt, j - 1] = pj[1]
            E = {0: (jnp.ones((8, 128), jnp.float32), jnp.zeros((8, 128), jnp.float32)), 1: e1}
            for b in range(2, 16):
                E[b] = cmul(E[b // 2], E[b - b // 2])
            R2[g, kt] = 2.0 * E[8][0]
            for b in range(16):
                if kt < 2:
                    SE[g, 2 * kt, b * 8:(b + 1) * 8, :] = E[b][0]
                    SE[g, 2 * kt + 1, b * 8:(b + 1) * 8, :] = E[b][1]
                else:
                    SE[g, 4, b * 8:(b + 1) * 8, :] = jnp.where(cosl, E[b][0], E[b][1])
    for f in range(16):
        for a in range(11):
            gf[a, f * LB:(f + 1) * LB, :] = grid[f, :, a * 128:(a + 1) * 128].astype(jnp.float32)

    lane16 = lax.broadcasted_iota(jnp.int32, (16, 128), 1)

    def row(ref, s):
        return jnp.broadcast_to(ref[pl.ds(s, 1), :], (8, 128))

    def table(g, s, t, kt):
        r2 = row(R2.at[g, kt], s)
        vs = [SE[g, t, pl.ds(s, 8, stride=8), :], SE[g, t, pl.ds(64 + s, 8, stride=8), :]]
        for b1 in range(2, 16):
            vs.append(r2 * vs[-1] - vs[-2])
        return jnp.concatenate(vs, axis=0).astype(jnp.bfloat16)

    def do_lat(l):
        g = l // 8
        s = l % 8
        lim = cnt[i * LB + l] - first
        rows = []
        for a in range(11):
            x = gf[a, pl.ds(l, 16, stride=LB), :]
            rows.append(jnp.where(lane16 < lim - 128 * a, x, 0.0).astype(jnp.bfloat16))
        lhs = jnp.concatenate(rows, axis=0)
        for kt in range(3):
            if kt < 2:
                tab = jnp.concatenate([table(g, s, 2 * kt, kt), table(g, s, 2 * kt + 1, kt)], axis=1)
            else:
                tab = table(g, s, 4, 2)
            y = jnp.dot(lhs, tab, preferred_element_type=jnp.float32)
            wc = row(WC.at[g, kt], s)
            ws = row(WS.at[g, kt], s)
            oc = [row(OC.at[g, kt, j], s) for j in range(5)]
            os = [row(OS.at[g, kt, j], s) for j in range(5)]
            for h in range(2):
                def blk(a, t):
                    return y[a * 16 + h * 8:a * 16 + h * 8 + 8, t * 128:(t + 1) * 128]
                if kt < 2:
                    re = blk(5, 0)
                    im = blk(5, 1)
                    for j in range(1, 6):
                        cp, cm = blk(5 + j, 0), blk(5 - j, 0)
                        sp, sm = blk(5 + j, 1), blk(5 - j, 1)
                        re = re + (oc[j - 1] * (cp + cm) - os[j - 1] * (sp - sm))
                        im = im + (os[j - 1] * (cp - cm) + oc[j - 1] * (sp + sm))
                    ob[2 * kt, pl.ds(h * 8 * LB + l, 8, stride=LB), :] = re * wc - im * ws
                    ob[2 * kt + 1, pl.ds(h * 8 * LB + l, 8, stride=LB), :] = -(im * wc + re * ws)
                else:
                    u = blk(5, 0)
                    v = jnp.zeros_like(u)
                    for j in range(1, 6):
                        p, q = blk(5 + j, 0), blk(5 - j, 0)
                        u = u + oc[j - 1] * (p + q)
                        v = v + os[j - 1] * (p - q)
                    v = jnp.where(cosl, pltpu.roll(v, 126, 1), pltpu.roll(v, 2, 1))
                    z = jnp.where(cosl, u - v, -(u + v))
                    zs = jnp.where(cosl, pltpu.roll(z, 126, 1), pltpu.roll(z, 2, 1))
                    ob[4, pl.ds(h * 8 * LB + l, 8, stride=LB), :] = z * wc + zs * ws

    UN = 8
    def step(n, carry):
        for u in range(UN):
            do_lat(n * UN + u)
        return carry
    lax.fori_loop(0, LB // UN, step, 0)
    for f in range(16):
        for t in range(5):
            out[f, :, t * 128:(t + 1) * 128] = ob[t, f * LB:(f + 1) * LB, :].astype(jnp.bfloat16)


def fourier_local(grid, counts, waves, first):
    L = grid.shape[1]
    ccol = jnp.broadcast_to(counts.astype(jnp.float32)[:, None], (L, 128))
    f32 = jnp.float32
    return pl.pallas_call(
        kernel,
        grid=(L // LB,),
        in_specs=[
            pl.BlockSpec(memory_space=pltpu.SMEM),
            pl.BlockSpec(memory_space=pltpu.SMEM),
            pl.BlockSpec(memory_space=pltpu.VMEM),
            pl.BlockSpec(memory_space=pltpu.VMEM),
            pl.BlockSpec((16, LB, 1408), lambda i: (0, i, 0)),
        ],
        out_specs=pl.BlockSpec((16, LB, 640), lambda i: (0, i, 0)),
        out_shape=jax.ShapeDtypeStruct((16, L, 640), jnp.bfloat16),
        scratch_shapes=[
            pltpu.VMEM((11, 16 * LB, 128), f32),
            pltpu.VMEM((2, 5, 128, 128), f32),
            pltpu.VMEM((2, 3, 8, 128), f32),
            pltpu.VMEM((2, 3, 5, 8, 128), f32),
            pltpu.VMEM((2, 3, 5, 8, 128), f32),
            pltpu.VMEM((2, 3, 8, 128), f32),
            pltpu.VMEM((2, 3, 8, 128), f32),
            pltpu.VMEM((5, 16 * LB, 128), f32),
        ],
        compiler_params=pltpu.CompilerParams(vmem_limit_bytes=48 * 2**20),
        name="fourier",
    )(first[None].astype(jnp.int32), counts, ccol, waves[None, :], grid)


def k_layout(order):
    main = order[:, :8].reshape(256)
    mix = jnp.concatenate([order[:, 8:], order[:, 8:]], axis=1).reshape(128)
    return jnp.concatenate([main, mix])

def leg_kernel(split, polys, x, out):
    s = pl.program_id(0)
    xs = x[0]
    hi = xs.astype(jnp.bfloat16)
    lo = (xs - hi.astype(jnp.float32)).astype(jnp.bfloat16)
    z = jnp.concatenate([hi, lo], axis=0)
    y = lax.dot_general(z, polys[0], (((1,), (1,)), ((), ())), preferred_element_type=jnp.float32)
    y = y[:16] + y[16:]
    r = lax.broadcasted_iota(jnp.int32, (4, 321), 1)
    sp = split[s]
    first = r < sp
    d = jnp.where(first, r, r - sp)
    even = d % 2 == 0
    out[0] = jnp.where(even, jnp.where(first, y[0:4], y[4:8]), jnp.where(first, y[8:12], y[12:16]))

def legendre(split, polys, x):
    return pl.pallas_call(
        leg_kernel, grid=(5,),
        in_specs=[pl.BlockSpec(memory_space=pltpu.SMEM), pl.BlockSpec((1, 321, 2560), lambda s: (s, 0, 0)), pl.BlockSpec((1, 16, 2560), lambda s: (s, 0, 0))],
        out_specs=pl.BlockSpec((1, 4, 321), lambda s: (s, 0, 0)),
        out_shape=jax.ShapeDtypeStruct((5, 4, 321), jnp.float32),
        compiler_params=pltpu.CompilerParams(vmem_limit_bytes=32 * 2**20),
        name="legendre",
    )(split, polys, x)


def body(grid, cycle_points, pair_slot, polys):
    lat_index = lax.axis_index("lat")
    lon_index = lax.axis_index("lon")
    lats = grid.shape[1]
    counts = lax.dynamic_slice_in_dim(cycle_points, lat_index * lats, lats)
    order = jnp.stack([pair_slot, MW - 1 - pair_slot], axis=1).reshape(32, 10)
    waves = (M0 + k_layout(order)).astype(jnp.float32)
    part = fourier_local(grid, counts, waves, lon_index * grid.shape[2])
    got = lax.all_to_all(part, "lon", split_axis=0, concat_axis=0, tiled=True)
    total = got.reshape(8, 2, lats, 640).astype(jnp.float32).sum(0)
    main = total[..., :512].reshape(2, lats, 2, 2, 16, 8)
    main = jnp.transpose(main, (2, 4, 5, 3, 0, 1)).reshape(32, 8, 2, 2, lats)
    mix = jnp.transpose(total[..., 512:].reshape(2, lats, 32, 2, 2), (2, 4, 3, 0, 1))
    sent = jnp.concatenate([main, mix], axis=1)
    held = lax.all_to_all(sent, "lat", split_axis=0, concat_axis=0, tiled=True)
    north = held[:16]
    south = held[16:][::-1, ..., ::-1]
    folded = jnp.stack([north + south, north - south])
    folded = folded.reshape(2, 16, 5, 2, 2, 2, lats)
    x = jnp.transpose(folded, (2, 0, 3, 4, 5, 1, 6)).reshape(5, 16, 16 * lats)
    local = lax.dynamic_slice_in_dim(pair_slot, lat_index * 5, 5)
    y = legendre(MW - local, polys, x).reshape(5, 2, 2, ROWS)
    return jnp.transpose(y, (2, 0, 3, 1))


def solution(mesh):
    in_specs = (P(None, "lat", "lon"), P(), P(), P("lat", None, None))
    out_specs = P("lon", "lat", None, None)
    return jax.shard_map(body, mesh=mesh, in_specs=in_specs, out_specs=out_specs, check_vma=False)
```

```python
import math

import jax
import jax.numpy as jnp
from jax import lax
from jax.experimental import pallas as pl
from jax.experimental.pallas import tpu as pltpu
from jax.sharding import PartitionSpec as P

MW = 320
M0 = 2240
ROWS = 321
LB = 16
NB = 10
UN = 8
NLATDEV = 32
SEG = 1408
BF = jnp.bfloat16
F32 = jnp.float32
MESH = pl.DeviceIdType.MESH


def sincos_turn(u):
    x = (u - jnp.floor(u + 0.5)) * math.pi
    y = x * x
    s = x * (1.0 + y * (-1 / 6 + y * (1 / 120 + y * (-1 / 5040 + y * (1 / 362880 + y * (-1 / 39916800 + y * (1 / 6227020800)))))))
    c = 1.0 + y * (-1 / 2 + y * (1 / 24 + y * (-1 / 720 + y * (1 / 40320 + y * (-1 / 3628800 + y * (1 / 479001600))))))
    return 1.0 - 2.0 * s * s, 2.0 * s * c


def fmod(x, c):
    r = x - jnp.floor(x / c) * c
    r = jnp.where(r < 0, r + c, r)
    return jnp.where(r >= c, r - c, r)


def cmul(p, q):
    return (p[0] * q[0] - p[1] * q[1], p[0] * q[1] + p[1] * q[0])


def kernel(cnt, pairs, prow, grid, polys, out,
           gin, gf, mrow, SE, R2, OC, OS, WC, WS, ob, SF, SB, RA, RB, KP, SZ, RZ, TR, S3, R3, XA, XM, PV,
           gsem, psem, sa_s, sa_r, sb_s, sb_r, sz_s, sz_r, s3_s, s3_r):
    lat = lax.axis_index("lat")
    lon = lax.axis_index("lon")
    x = lax.rem(lon, 4)
    z = lon // 4
    right = z * 4 + lax.rem(x + 1, 4)
    left = z * 4 + lax.rem(x + 3, 4)
    across = (1 - z) * 4 + x
    south = lat // 16

    barrier = pltpu.get_barrier_semaphore()
    for peer in (right, left, across):
        pl.semaphore_signal(barrier, inc=1, device_id=(lat, peer), device_id_type=MESH)

    def greet(d, carry):
        pl.semaphore_signal(barrier, inc=1, device_id=(lax.rem(lat + d, NLATDEV), lon), device_id_type=MESH)
        return carry

    def grid_copy(n):
        src = n + south * (NB - 1 - 2 * n)
        return pltpu.make_async_copy(
            grid.at[:, pl.ds(pl.multiple_of(src * LB, LB), LB), :], gin.at[n], gsem.at[n])

    def load(n, carry):
        grid_copy(n).start()
        return carry

    lax.fori_loop(0, NB, load, 0)
    lax.fori_loop(1, NLATDEV, greet, 0)
    polys_copy = pltpu.make_async_copy(polys, PV, psem)
    polys_copy.start()

    lane = lax.broadcasted_iota(jnp.int32, (8, 128), 1)
    sub = lax.broadcasted_iota(jnp.int32, (8, 128), 0)
    lane16 = lax.broadcasted_iota(jnp.int32, (16, 128), 1)
    cosl = (lane % 4) < 2
    first = lon * SEG
    base = jnp.where(south == 1, NLATDEV - 1 - lat, lat) * (LB * NB)

    col = lax.broadcasted_iota(jnp.int32, (160, 384), 1)
    slot_of = jnp.where(col < 256, 5 * (col // 8) + (col % 8) // 2, 5 * ((col - 256) // 4) + 4)
    pick_slot = jnp.where(slot_of == lax.broadcasted_iota(jnp.int32, (160, 384), 0), 1.0, 0.0).astype(BF)
    held_pair = jnp.dot(jnp.broadcast_to(prow[...].astype(F32), (8, 160)).astype(BF), pick_slot, preferred_element_type=F32)
    col8 = lax.broadcasted_iota(jnp.int32, (8, 384), 1)
    mrow[...] = M0 + jnp.where(col8 % 2 == 0, held_pair, MW - 1 - held_pair)

    def row(ref, s):
        return jnp.broadcast_to(ref[pl.ds(s, 1), :], (8, 128))

    def seeds(n):
        for g in range(2):
            c = jnp.zeros((8, 128), F32)
            for j in range(8):
                c = jnp.where(sub == j, cnt[base + n * LB + g * 8 + j].astype(F32), c)
            for kt in range(3):
                m = mrow[:, kt * 128:(kt + 1) * 128]
                r1 = fmod(m, c)
                e1 = sincos_turn(r1 / c)
                rp = fmod(r1 * 128.0, c)
                p1 = sincos_turn(rp / c)
                r0 = fmod(rp * (lon * 11 + 5).astype(F32), c)
                w = sincos_turn(r0 / c)
                scale = jnp.where(2.0 * m < c, 1.0 / c, 0.0)
                WC[g, kt] = w[0] * scale
                ws = w[1] * scale
                WS[g, kt] = jnp.where(cosl, ws, -ws) if kt == 2 else ws
                pj = p1
                for j in range(5):
                    if j:
                        pj = cmul(pj, p1)
                    OC[g, kt, j] = pj[0]
                    OS[g, kt, j] = pj[1]
                E = [(jnp.ones((8, 128), F32), jnp.zeros((8, 128), F32)), e1]
                for b in range(2, 16):
                    E.append(cmul(E[b // 2], E[b - b // 2]))
                R2[g, kt] = 2.0 * E[8][0]
                for b in range(16):
                    if kt < 2:
                        SE[g, 2 * kt, b * 8:(b + 1) * 8, :] = E[b][0]
                        SE[g, 2 * kt + 1, b * 8:(b + 1) * 8, :] = E[b][1]
                    else:
                        SE[g, 4, b * 8:(b + 1) * 8, :] = jnp.where(cosl, E[b][0], E[b][1])

    def table(g, s, t, kt):
        r2 = row(R2.at[g, kt], s)
        vs = [SE[g, t, pl.ds(s, 8, stride=8), :], SE[g, t, pl.ds(64 + s, 8, stride=8), :]]
        for _ in range(2, 16):
            vs.append(r2 * vs[-1] - vs[-2])
        return jnp.concatenate(vs, axis=0).astype(BF)

    def one_cycle(n, g, s):
        l = g * 8 + s
        lsrc = l + south * (LB - 1 - 2 * l)
        lim = cnt[base + n * LB + l] - first
        rows = []
        for a in range(11):
            v = gf[a, pl.ds(lsrc, 16, stride=LB), :]
            rows.append(jnp.where(lane16 < lim - 128 * a, v, 0.0).astype(BF))
        lhs = jnp.concatenate(rows, axis=0)
        for kt in range(3):
            if kt < 2:
                tab = jnp.concatenate([table(g, s, 2 * kt, kt), table(g, s, 2 * kt + 1, kt)], axis=1)
            else:
                tab = table(g, s, 4, 2)
            y = jnp.dot(lhs, tab, preferred_element_type=F32)
            wc = row(WC.at[g, kt], s)
            ws = row(WS.at[g, kt], s)
            oc = [row(OC.at[g, kt, j], s) for j in range(5)]
            os = [row(OS.at[g, kt, j], s) for j in range(5)]
            for h in range(2):
                def blk(a, t):
                    return y[a * 16 + h * 8:a * 16 + h * 8 + 8, t * 128:(t + 1) * 128]
                place = pl.ds(h * 8 * LB + l, 8, stride=LB)
                if kt < 2:
                    re = blk(5, 0)
                    im = blk(5, 1)
                    for j in range(1, 6):
                        cp, cm = blk(5 + j, 0), blk(5 - j, 0)
                        sp, sm = blk(5 + j, 1), blk(5 - j, 1)
                        re = re + (oc[j - 1] * (cp + cm) - os[j - 1] * (sp - sm))
                        im = im + (os[j - 1] * (cp - cm) + oc[j - 1] * (sp + sm))
                    ob[2 * kt, place, :] = re * wc - im * ws
                    ob[2 * kt + 1, place, :] = -(im * wc + re * ws)
                else:
                    u = blk(5, 0)
                    v = jnp.zeros_like(u)
                    for j in range(1, 6):
                        p, q = blk(5 + j, 0), blk(5 - j, 0)
                        u = u + oc[j - 1] * (p + q)
                        v = v + os[j - 1] * (p - q)
                    v = jnp.where(cosl, pltpu.roll(v, 126, 1), pltpu.roll(v, 2, 1))
                    w = jnp.where(cosl, u - v, -(u + v))
                    wsw = jnp.where(cosl, pltpu.roll(w, 126, 1), pltpu.roll(w, 2, 1))
                    ob[4, place, :] = w * wc + wsw * ws

    def remote(src, dst, ssem, rsem, la, lo):
        return pltpu.make_async_remote_copy(
            src_ref=src, dst_ref=dst, send_sem=ssem, recv_sem=rsem, device_id=(la, lo), device_id_type=MESH)

    def copy_a(n, side):
        return remote(SB.at[n, 2, side], RA.at[n, side], sa_s.at[n, side], sa_r.at[n, side], lat, (right, left)[side])

    def copy_b(n, side):
        return remote(SB.at[n, 1 + 2 * side], RB.at[n, side], sb_s.at[n, side], sb_r.at[n, side], lat, (right, left)[side])

    def copy_z(n):
        return remote(SZ.at[n], RZ.at[n], sz_s.at[n], sz_r.at[n], lat, across)

    LO, HI = (0, 8, 16, 24, 40, 48), (8, 16, 24, 40, 48, 56)

    def copy_3(c, d):
        to = lax.rem(lat + d, NLATDEV)
        return remote(S3.at[to, LO[c]:HI[c], :], R3.at[lat, LO[c]:HI[c], :], s3_s.at[c, d - 1], s3_r.at[c, d - 1], to, lon)

    def stage_f(n):
        grid_copy(n).wait()

        seeds(n)
        for f in range(16):
            for a in range(11):
                gf[a, f * LB:(f + 1) * LB, :] = gin[n, f, :, a * 128:(a + 1) * 128].astype(F32)

        def part(g, carry):
            for u in range(UN):
                one_cycle(n, g, u)
            return carry

        lax.fori_loop(0, LB // UN, part, 0)
        for f in range(16):
            h, xd, i = f // 8, (f % 8) // 2, f % 2
            rel = lax.rem(xd + 4 - x, 4)
            for t in range(5):
                v = ob[t, f * LB:(f + 1) * LB, :]
                SF[n, rel, h, i * LB:(i + 1) * LB, t * 128:(t + 1) * 128] = v
                SB[n, rel, h, i * LB:(i + 1) * LB, t * 128:(t + 1) * 128] = v.astype(BF)

        @pl.when(n == 0)
        def _():
            pl.semaphore_wait(barrier, NLATDEV - 1 + 3)

        for side in range(2):
            copy_a(n, side).start()

    def stage_b(n):
        for side in range(2):
            copy_a(n, side).wait_recv()
            SB[n, 1 + 2 * side, side] = (SF[n, 1 + 2 * side, side] + RA[n, side].astype(F32)).astype(BF)
            copy_b(n, side).start()

    def stage_c(n):
        for side in range(2):
            copy_b(n, side).wait_recv()

        def total(h):
            return SF[n, 0, h] + RB[n, 0, h].astype(F32) + RB[n, 1, h].astype(F32)

        SZ[n] = total(1 - z).astype(BF)
        copy_z(n).start()
        KP[n] = total(z)

    def turn(t):
        return jnp.transpose(TR[t]).reshape(16, 8, 128)

    def send_chunk(c):
        mix = turn(4)
        for half in range(2):
            re, im = turn(2 * half), turn(2 * half + 1)
            for j in range(16):
                i = half * 16 + j
                if c < 4:
                    S3[i, LO[c]:LO[c] + 8, :] = jnp.where(lane < 64, re[j], pltpu.roll(im[j], 64, 1))
                    v = pltpu.roll(mix[i // 2], 4, 0) if i % 2 != c // 2 else mix[i // 2]
                    if c % 2:
                        v = pltpu.roll(v, 64, 1)
                    if c:
                        v = jnp.where((sub // 4 == c // 2) & (lane // 64 == c % 2), v, S3[i, 32:40, :])
                    S3[i, 32:40, :] = v
                else:
                    v = pltpu.roll(mix[i // 2], 4, 0) if i % 2 else mix[i // 2]
                    S3[i, LO[c]:HI[c], :] = jnp.where(
                        lane < 32, re[j], jnp.where(lane < 64, pltpu.roll(im[j], 32, 1), pltpu.roll(v, 64, 1)))

        def go(d, carry):
            copy_3(c, d).start()
            return carry

        lax.fori_loop(1, NLATDEV, go, 0)
        R3[lat, LO[c]:HI[c], :] = S3[lat, LO[c]:HI[c], :]

    def stage_d(n):
        copy_z(n).wait_recv()
        width = jnp.where(n < 8, 2 * LB, LB)
        for i in range(2):
            start = pl.multiple_of(i * width + jnp.where(n < 8, lax.rem(n, 2), 0) * LB, LB)
            for t in range(5):
                TR[t, pl.ds(start, LB), :] = (
                    KP[n, i * LB:(i + 1) * LB, t * 128:(t + 1) * 128]
                    + RZ[n, i * LB:(i + 1) * LB, t * 128:(t + 1) * 128].astype(F32))
        for c, last in enumerate((1, 3, 5, 7, 8, 9)):
            @pl.when(n == last)
            def _():
                send_chunk(c)

    def step(n, carry):
        @pl.when(n < NB)
        def _():
            stage_f(n)

        @pl.when((n >= 1) & (n < NB + 1))
        def _():
            stage_b(n - 1)

        def run(stage, lag):
            def upto(k):
                return jnp.clip(k - lag + jnp.where(k >= NB, 1, 0), 0, NB)

            def one(k, carry):
                stage(k)
                return carry

            lax.fori_loop(upto(n - 1), upto(n), one, 0)

        run(stage_c, 2)
        run(stage_d, 3)
        return carry

    lax.fori_loop(0, NB + 3, step, 0)

    for c in range(6):
        def got(d, carry):
            copy_3(c, d).wait_recv()
            return carry

        lax.fori_loop(1, NLATDEV, got, 0)
    polys_copy.wait()

    def roll(v, k):
        return pltpu.roll(v, k % 128, 1) if k % 128 else v

    def quad(qd, carry):
        for sa in range(2):
            def held(i, r):
                a = R3[qd * 4 + i, r:r + 8, :]
                b = R3[NLATDEV - 1 - (qd * 4 + i), r:r + 8, :]
                return a + b if sa == 0 else a - b

            def piece(i, c, f, q, o):
                if c == 4:
                    k = q * 32 + f * 16
                    return jnp.where(lane < o + 16, roll(held(i, 40), o - k), roll(held(i, 48), o + 16 - k))
                if q < 2:
                    return roll(held(i, 8 * c), o - (q * 64 + f * 32))
                v = held(i, 32)
                v = pltpu.roll(v, 4, 0) if c // 2 else v
                return roll(v, o - ((c % 2) * 64 + f * 32))

            for f in range(2):
                for q in range(3):
                    for t in range(5):
                        v = None
                        for o in range(4):
                            i, c = divmod(4 * t + o, 5)
                            w = piece(i, c, f, q, 32 * o)
                            v = w if o == 0 else jnp.where(lane < 32 * o, v, w)
                        if q < 2:
                            r = ((sa * 2 + f) * 2 + q) * 8
                            XA[qd * 5 + t, r:r + 8, :] = v
                        else:
                            r = (sa * 2 + f) * 8
                            XM[qd * 5 + t, r:r + 8, :] = v
        return carry

    lax.fori_loop(0, 4, quad, 0)

    def parts(v):
        hi = v.astype(BF)
        return hi, (v - hi.astype(F32)).astype(BF)

    rr = lax.broadcasted_iota(jnp.int32, (1, ROWS), 1)
    for s in range(5):
        tiles = []
        for t in range(20):
            if s < 4:
                v = jnp.concatenate([XA[t, pl.ds(2 * s + k, 8, stride=8), :] for k in range(2)], axis=0)
            else:
                v = XM[t]
            tiles.append(jnp.concatenate(parts(v), axis=0))
        zz = jnp.concatenate(tiles, axis=1)
        y = lax.dot_general(zz, PV[s], (((1,), (1,)), ((), ())), preferred_element_type=F32)
        half = zz.shape[0] // 2
        y = y[:half] + y[half:]
        sp = MW - pairs[lat * 5 + s]
        in_first = rr < sp
        even = jnp.where(in_first, rr, rr - sp) % 2 == 0

        def pick(k, sa, f, q):
            j = (k * 8 + sa * 4 + f * 2 + q) if s < 4 else ((sa * 2 + f) * 8 + q * 2 + k)
            return y[j:j + 1]

        for f in range(2):
            for q in range(2):
                out[s, f * 2 + q:f * 2 + q + 1, :] = jnp.where(
                    even, jnp.where(in_first, pick(0, 0, f, q), pick(1, 0, f, q)),
                    jnp.where(in_first, pick(0, 1, f, q), pick(1, 1, f, q)))

    def sent(n, carry):
        for side in range(2):
            copy_a(n, side).wait_send()
            copy_b(n, side).wait_send()
        copy_z(n).wait_send()
        return carry

    lax.fori_loop(0, NB, sent, 0)
    for c in range(6):
        def gone(d, carry):
            copy_3(c, d).wait_send()
            return carry

        lax.fori_loop(1, NLATDEV, gone, 0)


def transform(grid, counts, pairs, polys):
    V = pltpu.VMEM
    dma = pltpu.SemaphoreType.DMA
    return pl.pallas_call(
        kernel,
        in_specs=[
            pl.BlockSpec(memory_space=pltpu.SMEM),
            pl.BlockSpec(memory_space=pltpu.SMEM),
            pl.BlockSpec(memory_space=pltpu.VMEM),
            pl.BlockSpec(memory_space=pl.ANY),
            pl.BlockSpec(memory_space=pl.ANY),
        ],
        out_specs=pl.BlockSpec(memory_space=pltpu.VMEM),
        out_shape=jax.ShapeDtypeStruct((5, 4, ROWS), F32),
        scratch_shapes=[
            V((NB, 16, LB, SEG), BF),
            V((11, 16 * LB, 128), F32),
            V((8, 384), F32),
            V((2, 5, 128, 128), F32),
            V((2, 3, 8, 128), F32),
            V((2, 3, 5, 8, 128), F32),
            V((2, 3, 5, 8, 128), F32),
            V((2, 3, 8, 128), F32),
            V((2, 3, 8, 128), F32),
            V((5, 16 * LB, 128), F32),
            V((NB, 4, 2, 2 * LB, 640), F32),
            V((NB, 4, 2, 2 * LB, 640), BF),
            V((NB, 2, 2 * LB, 640), BF),
            V((NB, 2, 2, 2 * LB, 640), BF),
            V((NB, 2 * LB, 640), F32),
            V((NB, 2 * LB, 640), BF),
            V((NB, 2 * LB, 640), BF),
            V((5, 128, 128), F32),
            V((NLATDEV, 56, 128), F32),
            V((NLATDEV, 56, 128), F32),
            V((20, 64, 128), F32),
            V((20, 32, 128), F32),
            V((5, ROWS, 2560), BF),
            dma((NB,)), dma(()),
            dma((NB, 2)), dma((NB, 2)), dma((NB, 2)), dma((NB, 2)), dma((NB,)), dma((NB,)),
            dma((6, NLATDEV - 1)), dma((6, NLATDEV - 1)),
        ],
        compiler_params=pltpu.CompilerParams(
            vmem_limit_bytes=56 * 2**20, collective_id=0, has_side_effects=True),
        name="transform",
    )(counts, pairs, pairs[None, :], grid, polys)


def body(grid, cycle_points, pair_slot, polys):
    y = transform(grid, cycle_points, pair_slot, polys).reshape(5, 2, 2, ROWS)
    return jnp.transpose(y, (1, 0, 3, 2))


def solution(mesh):
    in_specs = (P(None, "lat", "lon"), P(), P(), P("lat", None, None))
    out_specs = P("lon", "lat", None, None)
    return jax.shard_map(body, mesh=mesh, in_specs=in_specs, out_specs=out_specs, check_vma=False)
```

```python
import math

import jax
import jax.numpy as jnp
from jax import lax
from jax.experimental import pallas as pl
from jax.experimental.pallas import tpu as pltpu
from jax.sharding import PartitionSpec as P

MW = 320
M0 = 2240
ROWS = 321
LB = 16
NB = 10
UN = 8
NLATDEV = 32
SEG = 1408
BF = jnp.bfloat16
F32 = jnp.float32
MESH = pl.DeviceIdType.MESH
STEPS = 32000.0


def sincos_turn(u):
    x = (u - jnp.floor(u + 0.5)) * math.pi
    y = x * x
    s = x * (1.0 + y * (-1 / 6 + y * (1 / 120 + y * (-1 / 5040 + y * (1 / 362880 + y * (-1 / 39916800 + y * (1 / 6227020800)))))))
    c = 1.0 + y * (-1 / 2 + y * (1 / 24 + y * (-1 / 720 + y * (1 / 40320 + y * (-1 / 3628800 + y * (1 / 479001600))))))
    return 1.0 - 2.0 * s * s, 2.0 * s * c


def fmod(x, c):
    r = x - jnp.floor(x / c) * c
    r = jnp.where(r < 0, r + c, r)
    return jnp.where(r >= c, r - c, r)


def cmul(p, q):
    return (p[0] * q[0] - p[1] * q[1], p[0] * q[1] + p[1] * q[0])


def kernel(cnt, pairs, prow, grid, polys, out,
           gin, gf, mrow, SE, R2, OC, OS, WC, WS, ob, SF, SB, RA, RB, KP, SZ, RZ, TR, MX, CD, S3, R3, RD, XA, XM, PV,
           gsem, psem, sa_s, sa_r, sb_s, sb_r, sz_s, sz_r, s3_s, s3_r):
    lat = lax.axis_index("lat")
    lon = lax.axis_index("lon")
    x = lax.rem(lon, 4)
    z = lon // 4
    right = z * 4 + lax.rem(x + 1, 4)
    left = z * 4 + lax.rem(x + 3, 4)
    across = (1 - z) * 4 + x
    south = lat // 16

    barrier = pltpu.get_barrier_semaphore()
    for peer in (right, left, across):
        pl.semaphore_signal(barrier, inc=1, device_id=(lat, peer), device_id_type=MESH)

    def greet(d, carry):
        pl.semaphore_signal(barrier, inc=1, device_id=(lax.rem(lat + d, NLATDEV), lon), device_id_type=MESH)
        return carry

    def grid_copy(n):
        src = n + south * (NB - 1 - 2 * n)
        return pltpu.make_async_copy(
            grid.at[:, pl.ds(pl.multiple_of(src * LB, LB), LB), :], gin.at[n], gsem.at[n])

    def load(n, carry):
        grid_copy(n).start()
        return carry

    lax.fori_loop(0, NB, load, 0)
    lax.fori_loop(1, NLATDEV, greet, 0)
    polys_copy = pltpu.make_async_copy(polys, PV, psem)
    polys_copy.start()

    lane = lax.broadcasted_iota(jnp.int32, (8, 128), 1)
    sub = lax.broadcasted_iota(jnp.int32, (8, 128), 0)
    lane16 = lax.broadcasted_iota(jnp.int32, (16, 128), 1)
    cosl = (lane % 4) < 2
    first = lon * SEG
    base = jnp.where(south == 1, NLATDEV - 1 - lat, lat) * (LB * NB)

    col = lax.broadcasted_iota(jnp.int32, (160, 384), 1)
    slot_of = jnp.where(col < 256, 5 * (col // 8) + (col % 8) // 2, 5 * ((col - 256) // 4) + 4)
    pick_slot = jnp.where(slot_of == lax.broadcasted_iota(jnp.int32, (160, 384), 0), 1.0, 0.0).astype(BF)
    held_pair = jnp.dot(jnp.broadcast_to(prow[...].astype(F32), (8, 160)).astype(BF), pick_slot, preferred_element_type=F32)
    col8 = lax.broadcasted_iota(jnp.int32, (8, 384), 1)
    mrow[...] = M0 + jnp.where(col8 % 2 == 0, held_pair, MW - 1 - held_pair)

    def row(ref, s):
        return jnp.broadcast_to(ref[pl.ds(s, 1), :], (8, 128))

    def seeds(n):
        for g in range(2):
            c = jnp.zeros((8, 128), F32)
            for j in range(8):
                c = jnp.where(sub == j, cnt[base + n * LB + g * 8 + j].astype(F32), c)
            for kt in range(3):
                m = mrow[:, kt * 128:(kt + 1) * 128]
                r1 = fmod(m, c)
                e1 = sincos_turn(r1 / c)
                rp = fmod(r1 * 128.0, c)
                p1 = sincos_turn(rp / c)
                r0 = fmod(rp * (lon * 11 + 5).astype(F32), c)
                w = sincos_turn(r0 / c)
                scale = jnp.where(2.0 * m < c, 1.0 / c, 0.0)
                WC[g, kt] = w[0] * scale
                ws = w[1] * scale
                WS[g, kt] = jnp.where(cosl, ws, -ws) if kt == 2 else ws
                pj = p1
                for j in range(5):
                    if j:
                        pj = cmul(pj, p1)
                    OC[g, kt, j] = pj[0]
                    OS[g, kt, j] = pj[1]
                E = [(jnp.ones((8, 128), F32), jnp.zeros((8, 128), F32)), e1]
                for b in range(2, 16):
                    E.append(cmul(E[b // 2], E[b - b // 2]))
                R2[g, kt] = 2.0 * E[8][0]
                for b in range(16):
                    if kt < 2:
                        SE[g, 2 * kt, b * 8:(b + 1) * 8, :] = E[b][0]
                        SE[g, 2 * kt + 1, b * 8:(b + 1) * 8, :] = E[b][1]
                    else:
                        SE[g, 4, b * 8:(b + 1) * 8, :] = jnp.where(cosl, E[b][0], E[b][1])

    def table(g, s, t, kt):
        r2 = row(R2.at[g, kt], s)
        vs = [SE[g, t, pl.ds(s, 8, stride=8), :], SE[g, t, pl.ds(64 + s, 8, stride=8), :]]
        for _ in range(2, 16):
            vs.append(r2 * vs[-1] - vs[-2])
        return jnp.concatenate(vs, axis=0).astype(BF)

    def one_cycle(n, g, s):
        l = g * 8 + s
        lsrc = l + south * (LB - 1 - 2 * l)
        lim = cnt[base + n * LB + l] - first
        rows = []
        for a in range(11):
            v = gf[a, pl.ds(lsrc, 16, stride=LB), :]
            rows.append(jnp.where(lane16 < lim - 128 * a, v, 0.0).astype(BF))
        lhs = jnp.concatenate(rows, axis=0)
        for kt in range(3):
            if kt < 2:
                tab = jnp.concatenate([table(g, s, 2 * kt, kt), table(g, s, 2 * kt + 1, kt)], axis=1)
            else:
                tab = table(g, s, 4, 2)
            y = jnp.dot(lhs, tab, preferred_element_type=F32)
            wc = row(WC.at[g, kt], s)
            ws = row(WS.at[g, kt], s)
            oc = [row(OC.at[g, kt, j], s) for j in range(5)]
            os = [row(OS.at[g, kt, j], s) for j in range(5)]
            for h in range(2):
                def blk(a, t):
                    return y[a * 16 + h * 8:a * 16 + h * 8 + 8, t * 128:(t + 1) * 128]
                place = pl.ds(h * 8 * LB + l, 8, stride=LB)
                if kt < 2:
                    re = blk(5, 0)
                    im = blk(5, 1)
                    for j in range(1, 6):
                        cp, cm = blk(5 + j, 0), blk(5 - j, 0)
                        sp, sm = blk(5 + j, 1), blk(5 - j, 1)
                        re = re + (oc[j - 1] * (cp + cm) - os[j - 1] * (sp - sm))
                        im = im + (os[j - 1] * (cp - cm) + oc[j - 1] * (sp + sm))
                    ob[2 * kt, place, :] = re * wc - im * ws
                    ob[2 * kt + 1, place, :] = -(im * wc + re * ws)
                else:
                    u = blk(5, 0)
                    v = jnp.zeros_like(u)
                    for j in range(1, 6):
                        p, q = blk(5 + j, 0), blk(5 - j, 0)
                        u = u + oc[j - 1] * (p + q)
                        v = v + os[j - 1] * (p - q)
                    v = jnp.where(cosl, pltpu.roll(v, 126, 1), pltpu.roll(v, 2, 1))
                    w = jnp.where(cosl, u - v, -(u + v))
                    wsw = jnp.where(cosl, pltpu.roll(w, 126, 1), pltpu.roll(w, 2, 1))
                    ob[4, place, :] = w * wc + wsw * ws

    def remote(src, dst, ssem, rsem, la, lo):
        return pltpu.make_async_remote_copy(
            src_ref=src, dst_ref=dst, send_sem=ssem, recv_sem=rsem, device_id=(la, lo), device_id_type=MESH)

    def copy_a(n, side):
        return remote(SB.at[n, 2, side], RA.at[n, side], sa_s, sa_r.at[n, side], lat, (right, left)[side])

    def copy_b(n, side):
        return remote(SB.at[n, 1 + 2 * side], RB.at[n, side], sb_s, sb_r.at[n, side], lat, (right, left)[side])

    def copy_z(n):
        return remote(SZ.at[n], RZ.at[n], sz_s, sz_r.at[n], lat, across)

    LO, HI = (0, 16, 48), (16, 48, 64)

    def copy_3(c, d):
        to = lax.rem(lat + d, NLATDEV)
        return remote(S3.at[to, LO[c]:HI[c], :], R3.at[lat, LO[c]:HI[c], :], s3_s, s3_r.at[c // 2], to, lon)

    def stage_f(n):
        grid_copy(n).wait()

        seeds(n)
        for f in range(16):
            for a in range(11):
                gf[a, f * LB:(f + 1) * LB, :] = gin[n, f, :, a * 128:(a + 1) * 128].astype(F32)

        def part(g, carry):
            for u in range(UN):
                one_cycle(n, g, u)
            return carry

        lax.fori_loop(0, LB // UN, part, 0)
        for f in range(16):
            h, xd, i = f // 8, (f % 8) // 2, f % 2
            rel = lax.rem(xd + 4 - x, 4)
            for t in range(5):
                v = ob[t, f * LB:(f + 1) * LB, :]
                SF[n, rel, h, i * LB:(i + 1) * LB, t * 128:(t + 1) * 128] = v
                SB[n, rel, h, i * LB:(i + 1) * LB, t * 128:(t + 1) * 128] = v.astype(BF)

        @pl.when(n == 0)
        def _():
            pl.semaphore_wait(barrier, NLATDEV - 1 + 3)

        for side in range(2):
            copy_a(n, side).start()

    def stage_b(n):
        for side in range(2):
            copy_a(n, side).wait_recv()
            SB[n, 1 + 2 * side, side] = (SF[n, 1 + 2 * side, side] + RA[n, side].astype(F32)).astype(BF)
            copy_b(n, side).start()

    def stage_c(n):
        for side in range(2):
            copy_b(n, side).wait_recv()

        def total(h):
            return SF[n, 0, h] + RB[n, 0, h].astype(F32) + RB[n, 1, h].astype(F32)

        SZ[n] = total(1 - z).astype(BF)
        copy_z(n).start()
        KP[n] = total(z)

    def turn(t):
        return jnp.transpose(TR[t]).reshape(16, 8, 128)

    def send_chunk(c):
        ts = [turn(t) for t in range(5)]
        top = jnp.zeros((8, 128), F32)
        for v in ts:
            top = jnp.maximum(top, jnp.max(jnp.abs(v), axis=0))
        top = jnp.broadcast_to(jnp.max(top, axis=0, keepdims=True), (8, 128))
        code = jnp.ceil(jnp.log2(jnp.maximum(top, 1e-30)) * 64.0)
        inv = STEPS * jnp.exp2(code * (-1.0 / 64.0))
        qs = [jnp.floor(v * inv + 0.5) for v in ts]

        def put(i, r, upper, lower):
            S3[i, r:r + 16, :] = jnp.concatenate([upper, lower], axis=0).astype(jnp.int32).astype(jnp.int16)

        if c == 0:
            MX[...] = qs[4]
            CD[...] = code
        for i in range(NLATDEV):
            half, j = i // 16, i % 16
            re, im = qs[2 * half][j], qs[2 * half + 1][j]
            mix = pltpu.roll(qs[4][i // 2], 4, 0) if i % 2 != c % 2 else qs[4][i // 2]
            if c < 2:
                put(i, LO[c], re, im)
            if c == 1:
                mix0 = pltpu.roll(MX[i // 2], 4, 0) if i % 2 else MX[i // 2]
                put(i, 32, jnp.where(sub < 4, mix0, mix), jnp.where(sub == 0, CD[...], code))
            if c == 2:
                put(i, 48, jnp.where(lane < 64, re, pltpu.roll(mix, 64, 1)), jnp.where(lane < 64, im, pltpu.roll(code, 64, 1)))

        def go(d, carry):
            copy_3(c, d).start()
            return carry

        lax.fori_loop(1, NLATDEV, go, 0)
        R3[lat, LO[c]:HI[c], :] = S3[lat, LO[c]:HI[c], :]

    def stage_d(n):
        copy_z(n).wait_recv()
        width = jnp.where(n < 8, 4 * LB, 2 * LB)
        for i in range(2):
            start = pl.multiple_of(i * width + lax.rem(n, 4) * LB, LB)
            for t in range(5):
                TR[t, pl.ds(start, LB), :] = (
                    KP[n, i * LB:(i + 1) * LB, t * 128:(t + 1) * 128]
                    + RZ[n, i * LB:(i + 1) * LB, t * 128:(t + 1) * 128].astype(F32))
        for c, last in enumerate((3, 7, 9)):
            @pl.when(n == last)
            def _():
                send_chunk(c)

    def step(n, carry):
        @pl.when(n < NB)
        def _():
            stage_f(n)

        @pl.when((n >= 1) & (n < NB))
        def _():
            stage_b(n - 1)

        def run(stage, lag):
            def upto(k):
                return jnp.clip(k - lag, 0, NB)

            def one(k, carry):
                stage(k)
                return carry

            lax.fori_loop(upto(n - 1), upto(n), one, 0)

        run(stage_c, 2)
        run(stage_d, 3)

        @pl.when(n == NB)
        def _():
            stage_b(n - 1)

        return carry

    lax.fori_loop(0, NB + 4, step, 0)

    def drained(ref, sem):
        pltpu.make_async_copy(ref, ref, sem).wait()

    drained(RA, sa_s)
    drained(RB, sb_s)
    drained(SZ, sz_s)
    others = pl.ds(0, NLATDEV - 1)
    drained(S3.at[others], s3_s)
    polys_copy.wait()
    drained(R3.at[others, 0:48, :], s3_r.at[0])

    def roll(v, k):
        return pltpu.roll(v, k % 128, 1) if k % 128 else v

    def scale(v):
        return jnp.exp2(v * (1.0 / 64.0)) * (1.0 / STEPS)

    def take(i, r):
        v = R3[i, r:r + 16, :].astype(jnp.int32).astype(F32)
        return v[:8], v[8:]

    def fold(i, r, sa):
        a = RD[i, r:r + 8, :]
        b = RD[NLATDEV - 1 - i, r:r + 8, :]
        return a + b if sa == 0 else a - b

    def rows_of(sa, f, q):
        return (XA, ((sa * 2 + f) * 2 + q) * 8) if q < 2 else (XM, (sa * 2 + f) * 8)

    def decode_main(i, carry):
        mix, codes = take(i, 32)
        s0 = scale(jnp.broadcast_to(codes[0:1], (8, 128)))
        s1 = scale(jnp.broadcast_to(codes[1:2], (8, 128)))
        for r, sc in ((0, s0), (16, s1)):
            re, im = take(i, r)
            RD[i, r:r + 8, :] = re * sc
            RD[i, r + 8:r + 16, :] = im * sc
        RD[i, 32:40, :] = mix * jnp.where(sub < 4, s0, s1)
        return carry

    def quad_main(qd, carry):
        for sa in range(2):
            for f in range(2):
                for q in range(3):
                    v = []
                    for i in range(4):
                        if q < 2:
                            c0, c1 = fold(qd * 4 + i, q * 8, sa), fold(qd * 4 + i, 16 + q * 8, sa)
                        else:
                            c0 = fold(qd * 4 + i, 32, sa)
                            c1 = pltpu.roll(c0, 4, 0)
                        w = jnp.where(lane < 64, c0, roll(c1, 64)) if f == 0 else jnp.where(lane < 64, roll(c0, 64), c1)
                        v.append(roll(w, 32 * i))
                    ref, r = rows_of(sa, f, q)
                    ref[qd * 5, r:r + 8, :] = v[0]
                    ref[qd * 5 + 1, r:r + 8, :] = v[1]
                    ref[qd * 5 + 2, r:r + 8, :] = jnp.where(lane < 32, v[1], v[2])
                    ref[qd * 5 + 3, r:r + 8, :] = jnp.where(lane < 64, v[2], v[3])
                    ref[qd * 5 + 4, r:r + 8, :] = v[3]
        return carry

    lax.fori_loop(0, NLATDEV, decode_main, 0)
    lax.fori_loop(0, 4, quad_main, 0)

    drained(R3.at[others, 48:64, :], s3_r.at[1])

    def decode_rest(i, carry):
        upper, lower = take(i, 48)
        s2 = scale(jnp.where(lane < 64, pltpu.roll(lower, 64, 1), lower))
        RD[i, 40:48, :] = upper * s2
        RD[i, 48:56, :] = lower * s2
        return carry

    def quad_rest(qd, carry):
        for sa in range(2):
            for i in range(4):
                re, im = fold(qd * 4 + i, 40, sa), fold(qd * 4 + i, 48, sa)
                for f in range(2):
                    for q in range(3):
                        w = roll((re, im, re)[q], 32 * i - 32 * f - (64 if q == 2 else 0))
                        ref, r = rows_of(sa, f, q)
                        ref[qd * 5 + i + 1, r:r + 8, :] = jnp.where(lane // 32 == i, w, ref[qd * 5 + i + 1, r:r + 8, :])
        return carry

    lax.fori_loop(0, NLATDEV, decode_rest, 0)
    lax.fori_loop(0, 4, quad_rest, 0)

    def parts(v):
        hi = v.astype(BF)
        return hi, (v - hi.astype(F32)).astype(BF)

    rr = lax.broadcasted_iota(jnp.int32, (1, ROWS), 1)
    for s in range(5):
        tiles = []
        for t in range(20):
            if s < 4:
                v = jnp.concatenate([XA[t, pl.ds(2 * s + k, 8, stride=8), :] for k in range(2)], axis=0)
            else:
                v = XM[t]
            tiles.append(jnp.concatenate(parts(v), axis=0))
        zz = jnp.concatenate(tiles, axis=1)
        y = lax.dot_general(zz, PV[s], (((1,), (1,)), ((), ())), preferred_element_type=F32)
        half = zz.shape[0] // 2
        y = y[:half] + y[half:]
        sp = MW - pairs[lat * 5 + s]
        in_first = rr < sp
        even = jnp.where(in_first, rr, rr - sp) % 2 == 0

        def pick(k, sa, f, q):
            j = (k * 8 + sa * 4 + f * 2 + q) if s < 4 else ((sa * 2 + f) * 8 + q * 2 + k)
            return y[j:j + 1]

        for f in range(2):
            for q in range(2):
                out[s, f * 2 + q:f * 2 + q + 1, :] = jnp.where(
                    even, jnp.where(in_first, pick(0, 0, f, q), pick(1, 0, f, q)),
                    jnp.where(in_first, pick(0, 1, f, q), pick(1, 1, f, q)))


def transform(grid, counts, pairs, polys):
    V = pltpu.VMEM
    dma = pltpu.SemaphoreType.DMA
    return pl.pallas_call(
        kernel,
        in_specs=[
            pl.BlockSpec(memory_space=pltpu.SMEM),
            pl.BlockSpec(memory_space=pltpu.SMEM),
            pl.BlockSpec(memory_space=pltpu.VMEM),
            pl.BlockSpec(memory_space=pl.ANY),
            pl.BlockSpec(memory_space=pl.ANY),
        ],
        out_specs=pl.BlockSpec(memory_space=pltpu.VMEM),
        out_shape=jax.ShapeDtypeStruct((5, 4, ROWS), F32),
        scratch_shapes=[
            V((NB, 16, LB, SEG), BF),
            V((11, 16 * LB, 128), F32),
            V((8, 384), F32),
            V((2, 5, 128, 128), F32),
            V((2, 3, 8, 128), F32),
            V((2, 3, 5, 8, 128), F32),
            V((2, 3, 5, 8, 128), F32),
            V((2, 3, 8, 128), F32),
            V((2, 3, 8, 128), F32),
            V((5, 16 * LB, 128), F32),
            V((NB, 4, 2, 2 * LB, 640), F32),
            V((NB, 4, 2, 2 * LB, 640), BF),
            V((NB, 2, 2 * LB, 640), BF),
            V((NB, 2, 2, 2 * LB, 640), BF),
            V((NB, 2 * LB, 640), F32),
            V((NB, 2 * LB, 640), BF),
            V((NB, 2 * LB, 640), BF),
            V((5, 128, 128), F32),
            V((16, 8, 128), F32),
            V((8, 128), F32),
            V((NLATDEV, 64, 128), jnp.int16),
            V((NLATDEV, 64, 128), jnp.int16),
            V((NLATDEV, 56, 128), F32),
            V((20, 64, 128), F32),
            V((20, 32, 128), F32),
            V((5, ROWS, 2560), BF),
            dma((NB,)), dma(()),
            dma(()), dma((NB, 2)), dma(()), dma((NB, 2)), dma(()), dma((NB,)),
            dma(()), dma((2,)),
        ],
        compiler_params=pltpu.CompilerParams(
            vmem_limit_bytes=56 * 2**20, collective_id=0, has_side_effects=True),
        name="transform",
    )(counts, pairs, pairs[None, :], grid, polys)


def body(grid, cycle_points, pair_slot, polys):
    y = transform(grid, cycle_points, pair_slot, polys).reshape(5, 2, 2, ROWS)
    return jnp.transpose(y, (1, 0, 3, 2))


def solution(mesh):
    in_specs = (P(None, "lat", "lon"), P(), P(), P("lat", None, None))
    out_specs = P("lon", "lat", None, None)
    return jax.shard_map(body, mesh=mesh, in_specs=in_specs, out_specs=out_specs, check_vma=False)
```

```python
import math

import jax
import jax.numpy as jnp
from jax import lax
from jax.experimental import pallas as pl
from jax.experimental.pallas import tpu as pltpu
from jax.sharding import PartitionSpec as P

MW = 320
M0 = 2240
ROWS = 321
LB = 16
GS = 24
NB = 10
UN = 8
NLATDEV = 32
SEG = 1408
BF = jnp.bfloat16
F32 = jnp.float32
MESH = pl.DeviceIdType.MESH
STEPS = 32000.0


def sincos_turn(u):
    x = (u - jnp.floor(u + 0.5)) * math.pi
    y = x * x
    s = x * (1.0 + y * (-1 / 6 + y * (1 / 120 + y * (-1 / 5040 + y * (1 / 362880 + y * (-1 / 39916800 + y * (1 / 6227020800)))))))
    c = 1.0 + y * (-1 / 2 + y * (1 / 24 + y * (-1 / 720 + y * (1 / 40320 + y * (-1 / 3628800 + y * (1 / 479001600))))))
    return 1.0 - 2.0 * s * s, 2.0 * s * c


def fmod(x, c):
    r = x - jnp.floor(x / c) * c
    r = jnp.where(r < 0, r + c, r)
    return jnp.where(r >= c, r - c, r)


def cmul(p, q):
    return (p[0] * q[0] - p[1] * q[1], p[0] * q[1] + p[1] * q[0])


def kernel(cnt, pairs, prow, grid, polys, out,
           gin, gf, mrow, SE, R2, OC, OS, WC, WS, ob, SF, SB, RA, RB, KP, SZ, RZ, TR, MX, CD, S3, R3, RD, XA, XM, PV,
           gsem, psem, sa_s, sa_r, sb_s, sb_r, sz_s, sz_r, s3_s, s3_r):
    lat = lax.axis_index("lat")
    lon = lax.axis_index("lon")
    x = lax.rem(lon, 4)
    z = lon // 4
    right = z * 4 + lax.rem(x + 1, 4)
    left = z * 4 + lax.rem(x + 3, 4)
    across = (1 - z) * 4 + x
    south = lat // 16

    barrier = pltpu.get_barrier_semaphore()
    for peer in (right, left, across):
        pl.semaphore_signal(barrier, inc=1, device_id=(lat, peer), device_id_type=MESH)

    def greet(d, carry):
        pl.semaphore_signal(barrier, inc=1, device_id=(lax.rem(lat + d, NLATDEV), lon), device_id_type=MESH)
        return carry

    def grid_copy(n):
        src = n + south * (NB - 1 - 2 * n)
        return pltpu.make_async_copy(
            grid.at[:, pl.ds(pl.multiple_of(src * LB, LB), LB), :], gin.at[n], gsem.at[n])

    def load(n, carry):
        grid_copy(n).start()
        return carry

    lax.fori_loop(0, NB, load, 0)
    lax.fori_loop(1, NLATDEV, greet, 0, unroll=True)
    polys_copy = pltpu.make_async_copy(polys, PV, psem)
    polys_copy.start()

    lane = lax.broadcasted_iota(jnp.int32, (8, 128), 1)
    sub = lax.broadcasted_iota(jnp.int32, (8, 128), 0)
    lane16 = lax.broadcasted_iota(jnp.int32, (16, 128), 1)
    cosl = (lane % 4) < 2
    first = lon * SEG
    base = jnp.where(south == 1, NLATDEV - 1 - lat, lat) * (LB * NB)

    col = lax.broadcasted_iota(jnp.int32, (160, 384), 1)
    slot_of = jnp.where(col < 256, 5 * (col // 8) + (col % 8) // 2, 5 * ((col - 256) // 4) + 4)
    pick_slot = jnp.where(slot_of == lax.broadcasted_iota(jnp.int32, (160, 384), 0), 1.0, 0.0).astype(BF)
    held_pair = jnp.dot(jnp.broadcast_to(prow[...].astype(F32), (8, 160)).astype(BF), pick_slot, preferred_element_type=F32)
    col8 = lax.broadcasted_iota(jnp.int32, (8, 384), 1)
    mrow[...] = M0 + jnp.where(col8 % 2 == 0, held_pair, MW - 1 - held_pair)

    def row(ref, s):
        return jnp.broadcast_to(ref[pl.ds(s, 1), :], (8, 128))

    def seeds(n):
        for g in range(2):
            c = jnp.zeros((8, 128), F32)
            for j in range(8):
                c = jnp.where(sub == j, cnt[base + n * LB + g * 8 + j].astype(F32), c)
            for kt in range(3):
                m = mrow[:, kt * 128:(kt + 1) * 128]
                r1 = fmod(m, c)
                e1 = sincos_turn(r1 / c)
                rp = fmod(r1 * 128.0, c)
                p1 = sincos_turn(rp / c)
                r0 = fmod(rp * (lon * 11 + 5).astype(F32), c)
                w = sincos_turn(r0 / c)
                scale = jnp.where(2.0 * m < c, 1.0 / c, 0.0)
                WC[g, kt] = w[0] * scale
                ws = w[1] * scale
                WS[g, kt] = jnp.where(cosl, ws, -ws) if kt == 2 else ws
                pj = p1
                for j in range(5):
                    if j:
                        pj = cmul(pj, p1)
                    OC[g, kt, j] = pj[0]
                    OS[g, kt, j] = pj[1]
                E = [(jnp.ones((8, 128), F32), jnp.zeros((8, 128), F32)), e1]
                for b in range(2, 16):
                    E.append(cmul(E[b // 2], E[b - b // 2]))
                R2[g, kt] = 2.0 * E[8][0]
                for b in range(16):
                    if kt < 2:
                        SE[g, 2 * kt, b * 8:(b + 1) * 8, :] = E[b][0]
                        SE[g, 2 * kt + 1, b * 8:(b + 1) * 8, :] = E[b][1]
                    else:
                        SE[g, 4, b * 8:(b + 1) * 8, :] = jnp.where(cosl, E[b][0], E[b][1])

    def table(g, s, t, kt):
        r2 = row(R2.at[g, kt], s)
        vs = [SE[g, t, pl.ds(s, 8, stride=8), :], SE[g, t, pl.ds(64 + s, 8, stride=8), :]]
        for _ in range(2, 16):
            vs.append(r2 * vs[-1] - vs[-2])
        return jnp.concatenate(vs, axis=0).astype(BF)

    def one_cycle(n, g, s):
        l = g * 8 + s
        lsrc = l + south * (LB - 1 - 2 * l)
        lim = cnt[base + n * LB + l] - first
        rows = []
        for a in range(11):
            v = gf[a, pl.ds(lsrc, 16, stride=GS), :]
            rows.append(jnp.where(lane16 < lim - 128 * a, v, 0.0).astype(BF))
        lhs = jnp.concatenate(rows, axis=0)
        for kt in range(3):
            if kt < 2:
                tab = jnp.concatenate([table(g, s, 2 * kt, kt), table(g, s, 2 * kt + 1, kt)], axis=1)
            else:
                tab = table(g, s, 4, 2)
            y = jnp.dot(lhs, tab, preferred_element_type=F32)
            wc = row(WC.at[g, kt], s)
            ws = row(WS.at[g, kt], s)
            oc = [row(OC.at[g, kt, j], s) for j in range(5)]
            os = [row(OS.at[g, kt, j], s) for j in range(5)]
            for h in range(2):
                def blk(a, t):
                    return y[a * 16 + h * 8:a * 16 + h * 8 + 8, t * 128:(t + 1) * 128]
                place = pl.ds(h * 8 * GS + l, 8, stride=GS)
                if kt < 2:
                    re = blk(5, 0)
                    im = blk(5, 1)
                    for j in range(1, 6):
                        cp, cm = blk(5 + j, 0), blk(5 - j, 0)
                        sp, sm = blk(5 + j, 1), blk(5 - j, 1)
                        re = re + (oc[j - 1] * (cp + cm) - os[j - 1] * (sp - sm))
                        im = im + (os[j - 1] * (cp - cm) + oc[j - 1] * (sp + sm))
                    ob[2 * kt, place, :] = re * wc - im * ws
                    ob[2 * kt + 1, place, :] = -(im * wc + re * ws)
                else:
                    u = blk(5, 0)
                    v = jnp.zeros_like(u)
                    for j in range(1, 6):
                        p, q = blk(5 + j, 0), blk(5 - j, 0)
                        u = u + oc[j - 1] * (p + q)
                        v = v + os[j - 1] * (p - q)
                    v = jnp.where(cosl, pltpu.roll(v, 126, 1), pltpu.roll(v, 2, 1))
                    w = jnp.where(cosl, u - v, -(u + v))
                    wsw = jnp.where(cosl, pltpu.roll(w, 126, 1), pltpu.roll(w, 2, 1))
                    ob[4, place, :] = w * wc + wsw * ws

    def remote(src, dst, ssem, rsem, la, lo):
        return pltpu.make_async_remote_copy(
            src_ref=src, dst_ref=dst, send_sem=ssem, recv_sem=rsem, device_id=(la, lo), device_id_type=MESH)

    def copy_a(n, side):
        return remote(SB.at[n, 2, side], RA.at[n, side], sa_s, sa_r.at[n, side], lat, (right, left)[side])

    def copy_b(n, side):
        return remote(SB.at[n, 1 + 2 * side], RB.at[n, side], sb_s, sb_r.at[n, side], lat, (right, left)[side])

    def copy_z(n):
        return remote(SZ.at[n], RZ.at[n], sz_s, sz_r.at[n], lat, across)

    LO, HI = (0, 16, 48), (16, 48, 64)

    def copy_3(c, d):
        to = lax.rem(lat + d, NLATDEV)
        return remote(S3.at[to, LO[c]:HI[c], :], R3.at[lat, LO[c]:HI[c], :], s3_s, s3_r.at[c // 2], to, lon)

    def stage_f(n):
        grid_copy(n).wait()

        seeds(n)
        for f in range(16):
            for a in range(11):
                gf[a, f * GS:f * GS + LB, :] = gin[n, f, :, a * 128:(a + 1) * 128].astype(F32)

        def part(g, carry):
            for u in range(UN):
                one_cycle(n, g, u)
            return carry

        for u in range(LB):
            one_cycle(n, u // 8, u % 8)
        for f in range(16):
            h, xd, i = f // 8, (f % 8) // 2, f % 2
            rel = lax.rem(xd + 4 - x, 4)
            for t in range(5):
                v = ob[t, f * GS:f * GS + LB, :]
                SF[n, rel, h, i * LB:(i + 1) * LB, t * 128:(t + 1) * 128] = v
                SB[n, rel, h, i * LB:(i + 1) * LB, t * 128:(t + 1) * 128] = v.astype(BF)

        @pl.when(n == 0)
        def _():
            pl.semaphore_wait(barrier, NLATDEV - 1 + 3)

        for side in range(2):
            copy_a(n, side).start()

    def stage_b(n):
        for side in range(2):
            copy_a(n, side).wait_recv()
            SB[n, 1 + 2 * side, side] = (SF[n, 1 + 2 * side, side] + RA[n, side].astype(F32)).astype(BF)
            copy_b(n, side).start()

    def stage_c(n):
        for side in range(2):
            copy_b(n, side).wait_recv()

        def total(h):
            return SF[n, 0, h] + RB[n, 0, h].astype(F32) + RB[n, 1, h].astype(F32)

        SZ[n] = total(1 - z).astype(BF)
        copy_z(n).start()
        KP[n] = total(z)

    def turn(t):
        return jnp.transpose(TR[t]).reshape(16, 8, 128)

    def send_chunk(c):
        ts = [turn(t) for t in range(5)]
        top = jnp.zeros((8, 128), F32)
        for v in ts:
            top = jnp.maximum(top, jnp.max(jnp.abs(v), axis=0))
        top = jnp.broadcast_to(jnp.max(top, axis=0, keepdims=True), (8, 128))
        code = jnp.ceil(jnp.log2(jnp.maximum(top, 1e-30)) * 64.0)
        inv = STEPS * jnp.exp2(code * (-1.0 / 64.0))
        qs = [jnp.floor(v * inv + 0.5) for v in ts]

        def put(i, r, upper, lower):
            S3[i, r:r + 16, :] = jnp.concatenate([upper, lower], axis=0).astype(jnp.int32).astype(jnp.int16)

        if c == 0:
            MX[...] = qs[4]
            CD[...] = code
        for i in range(NLATDEV):
            half, j = i // 16, i % 16
            re, im = qs[2 * half][j], qs[2 * half + 1][j]
            mix = pltpu.roll(qs[4][i // 2], 4, 0) if i % 2 != c % 2 else qs[4][i // 2]
            if c < 2:
                put(i, LO[c], re, im)
            if c == 1:
                mix0 = pltpu.roll(MX[i // 2], 4, 0) if i % 2 else MX[i // 2]
                put(i, 32, jnp.where(sub < 4, mix0, mix), jnp.where(sub == 0, CD[...], code))
            if c == 2:
                put(i, 48, jnp.where(lane < 64, re, pltpu.roll(mix, 64, 1)), jnp.where(lane < 64, im, pltpu.roll(code, 64, 1)))

        def go(d, carry):
            copy_3(c, d).start()
            return carry

        lax.fori_loop(1, NLATDEV, go, 0, unroll=True)
        R3[lat, LO[c]:HI[c], :] = S3[lat, LO[c]:HI[c], :]

    def stage_d(n):
        copy_z(n).wait_recv()
        width = jnp.where(n < 8, 4 * LB, 2 * LB)
        for i in range(2):
            start = pl.multiple_of(i * width + lax.rem(n, 4) * LB, LB)
            for t in range(5):
                TR[t, pl.ds(start, LB), :] = (
                    KP[n, i * LB:(i + 1) * LB, t * 128:(t + 1) * 128]
                    + RZ[n, i * LB:(i + 1) * LB, t * 128:(t + 1) * 128].astype(F32))
        for c, last in enumerate((3, 7, 9)):
            @pl.when(n == last)
            def _():
                send_chunk(c)

    def step(n, carry):
        @pl.when(n < NB)
        def _():
            stage_f(n)

        @pl.when((n >= 2) & (n < NB))
        def _():
            stage_b(n - 2)

        def run(stage, lag):
            def upto(k):
                return jnp.clip(k - lag, 0, NB)

            def one(k, carry):
                stage(k)
                return carry

            lax.fori_loop(upto(n - 1), upto(n), one, 0)

        run(stage_c, 3)
        run(stage_d, 4)

        @pl.when(n == NB)
        def _():
            stage_b(n - 2)
            stage_b(n - 1)

        return carry

    lax.fori_loop(0, NB + 5, step, 0)

    def drained(ref, sem):
        pltpu.make_async_copy(ref, ref, sem).wait()

    drained(RA, sa_s)
    drained(RB, sb_s)
    drained(SZ, sz_s)
    others = pl.ds(0, NLATDEV - 1)
    drained(S3.at[others], s3_s)
    polys_copy.wait()
    drained(R3.at[others, 0:48, :], s3_r.at[0])

    def roll(v, k):
        return pltpu.roll(v, k % 128, 1) if k % 128 else v

    def scale(v):
        return jnp.exp2(v * (1.0 / 64.0)) * (1.0 / STEPS)

    def take(i, r):
        v = R3[i, r:r + 16, :].astype(jnp.int32).astype(F32)
        return v[:8], v[8:]

    def fold(i, r, sa):
        a = RD[i, r:r + 8, :]
        b = RD[NLATDEV - 1 - i, r:r + 8, :]
        return a + b if sa == 0 else a - b

    def rows_of(sa, f, q):
        return (XA, ((sa * 2 + f) * 2 + q) * 8) if q < 2 else (XM, (sa * 2 + f) * 8)

    def decode_main(i, carry):
        mix, codes = take(i, 32)
        s0 = scale(jnp.broadcast_to(codes[0:1], (8, 128)))
        s1 = scale(jnp.broadcast_to(codes[1:2], (8, 128)))
        for r, sc in ((0, s0), (16, s1)):
            re, im = take(i, r)
            RD[i, r:r + 8, :] = re * sc
            RD[i, r + 8:r + 16, :] = im * sc
        RD[i, 32:40, :] = mix * jnp.where(sub < 4, s0, s1)
        return carry

    def quad_main(qd, carry):
        for sa in range(2):
            for f in range(2):
                for q in range(3):
                    v = []
                    for i in range(4):
                        if q < 2:
                            c0, c1 = fold(qd * 4 + i, q * 8, sa), fold(qd * 4 + i, 16 + q * 8, sa)
                        else:
                            c0 = fold(qd * 4 + i, 32, sa)
                            c1 = pltpu.roll(c0, 4, 0)
                        w = jnp.where(lane < 64, c0, roll(c1, 64)) if f == 0 else jnp.where(lane < 64, roll(c0, 64), c1)
                        v.append(roll(w, 32 * i))
                    ref, r = rows_of(sa, f, q)
                    ref[qd * 5, r:r + 8, :] = v[0]
                    ref[qd * 5 + 1, r:r + 8, :] = v[1]
                    ref[qd * 5 + 2, r:r + 8, :] = jnp.where(lane < 32, v[1], v[2])
                    ref[qd * 5 + 3, r:r + 8, :] = jnp.where(lane < 64, v[2], v[3])
                    ref[qd * 5 + 4, r:r + 8, :] = v[3]
        return carry

    lax.fori_loop(0, NLATDEV, decode_main, 0)
    lax.fori_loop(0, 4, quad_main, 0)

    drained(R3.at[others, 48:64, :], s3_r.at[1])

    def decode_rest(i, carry):
        upper, lower = take(i, 48)
        s2 = scale(jnp.where(lane < 64, pltpu.roll(lower, 64, 1), lower))
        RD[i, 40:48, :] = upper * s2
        RD[i, 48:56, :] = lower * s2
        return carry

    def quad_rest(qd, carry):
        for sa in range(2):
            for i in range(4):
                re, im = fold(qd * 4 + i, 40, sa), fold(qd * 4 + i, 48, sa)
                for f in range(2):
                    for q in range(3):
                        w = roll((re, im, re)[q], 32 * i - 32 * f - (64 if q == 2 else 0))
                        ref, r = rows_of(sa, f, q)
                        ref[qd * 5 + i + 1, r:r + 8, :] = jnp.where(lane // 32 == i, w, ref[qd * 5 + i + 1, r:r + 8, :])
        return carry

    lax.fori_loop(0, NLATDEV, decode_rest, 0)
    lax.fori_loop(0, 4, quad_rest, 0)

    def parts(v):
        hi = v.astype(BF)
        return hi, (v - hi.astype(F32)).astype(BF)

    rr = lax.broadcasted_iota(jnp.int32, (1, ROWS), 1)
    for s in range(5):
        tiles = []
        for t in range(20):
            if s < 4:
                v = jnp.concatenate([XA[t, pl.ds(2 * s + k, 8, stride=8), :] for k in range(2)], axis=0)
            else:
                v = XM[t]
            tiles.append(jnp.concatenate(parts(v), axis=0))
        zz = jnp.concatenate(tiles, axis=1)
        y = lax.dot_general(zz, PV[s], (((1,), (1,)), ((), ())), preferred_element_type=F32)
        half = zz.shape[0] // 2
        y = y[:half] + y[half:]
        sp = MW - pairs[lat * 5 + s]
        in_first = rr < sp
        even = jnp.where(in_first, rr, rr - sp) % 2 == 0

        def pick(k, sa, f, q):
            j = (k * 8 + sa * 4 + f * 2 + q) if s < 4 else ((sa * 2 + f) * 8 + q * 2 + k)
            return y[j:j + 1]

        for f in range(2):
            for q in range(2):
                out[f, s, q:q + 1, :] = jnp.where(
                    even, jnp.where(in_first, pick(0, 0, f, q), pick(1, 0, f, q)),
                    jnp.where(in_first, pick(0, 1, f, q), pick(1, 1, f, q)))


def transform(grid, counts, pairs, polys):
    V = pltpu.VMEM
    dma = pltpu.SemaphoreType.DMA
    return pl.pallas_call(
        kernel,
        in_specs=[
            pl.BlockSpec(memory_space=pltpu.SMEM),
            pl.BlockSpec(memory_space=pltpu.SMEM),
            pl.BlockSpec(memory_space=pltpu.VMEM),
            pl.BlockSpec(memory_space=pl.ANY),
            pl.BlockSpec(memory_space=pl.ANY),
        ],
        out_specs=pl.BlockSpec(memory_space=pltpu.VMEM),
        out_shape=jax.ShapeDtypeStruct((2, 5, 2, ROWS), F32),
        scratch_shapes=[
            V((NB, 16, LB, SEG), BF),
            V((11, 16 * GS, 128), F32),
            V((8, 384), F32),
            V((2, 5, 128, 128), F32),
            V((2, 3, 8, 128), F32),
            V((2, 3, 5, 8, 128), F32),
            V((2, 3, 5, 8, 128), F32),
            V((2, 3, 8, 128), F32),
            V((2, 3, 8, 128), F32),
            V((5, 16 * GS, 128), F32),
            V((NB, 4, 2, 2 * LB, 640), F32),
            V((NB, 4, 2, 2 * LB, 640), BF),
            V((NB, 2, 2 * LB, 640), BF),
            V((NB, 2, 2, 2 * LB, 640), BF),
            V((NB, 2 * LB, 640), F32),
            V((NB, 2 * LB, 640), BF),
            V((NB, 2 * LB, 640), BF),
            V((5, 128, 128), F32),
            V((16, 8, 128), F32),
            V((8, 128), F32),
            V((NLATDEV, 64, 128), jnp.int16),
            V((NLATDEV, 64, 128), jnp.int16),
            V((NLATDEV, 56, 128), F32),
            V((20, 64, 128), F32),
            V((20, 32, 128), F32),
            V((5, ROWS, 2560), BF),
            dma((NB,)), dma(()),
            dma(()), dma((NB, 2)), dma(()), dma((NB, 2)), dma(()), dma((NB,)),
            dma(()), dma((2,)),
        ],
        compiler_params=pltpu.CompilerParams(
            vmem_limit_bytes=56 * 2**20, collective_id=0, has_side_effects=True),
        name="transform",
    )(counts, pairs, pairs[None, :], grid, polys)


def body(grid, cycle_points, pair_slot, polys):
    return jnp.swapaxes(transform(grid, cycle_points, pair_slot, polys), 2, 3)


def solution(mesh):
    in_specs = (P(None, "lat", "lon"), P(), P(), P("lat", None, None))
    out_specs = P("lon", "lat", None, None)
    return jax.shard_map(body, mesh=mesh, in_specs=in_specs, out_specs=out_specs, check_vma=False)
```

```python
import math

import jax
import jax.numpy as jnp
from jax import lax
from jax.experimental import pallas as pl
from jax.experimental.pallas import tpu as pltpu
from jax.sharding import PartitionSpec as P

MW = 320
M0 = 2240
ROWS = 321
LB = 16
GS = 24
NB = 10
UN = 8
NLATDEV = 32
SEG = 1408
BF = jnp.bfloat16
F32 = jnp.float32
MESH = pl.DeviceIdType.MESH
STEPS = 32000.0


def sincos_turn(u):
    x = (u - jnp.floor(u + 0.5)) * math.pi
    y = x * x
    s = x * (1.0 + y * (-1 / 6 + y * (1 / 120 + y * (-1 / 5040 + y * (1 / 362880 + y * (-1 / 39916800 + y * (1 / 6227020800)))))))
    c = 1.0 + y * (-1 / 2 + y * (1 / 24 + y * (-1 / 720 + y * (1 / 40320 + y * (-1 / 3628800 + y * (1 / 479001600))))))
    return 1.0 - 2.0 * s * s, 2.0 * s * c


def fmod(x, c):
    r = x - jnp.floor(x / c) * c
    r = jnp.where(r < 0, r + c, r)
    return jnp.where(r >= c, r - c, r)


def cmul(p, q):
    return (p[0] * q[0] - p[1] * q[1], p[0] * q[1] + p[1] * q[0])


def kernel(cnt, pairs, prow, grid, polys, out,
           gin, gf, mrow, SE, R2, OC, OS, WC, WS, ob, SF, SB, RA, RB, KP, SZ, RZ, TR, MX, CD, S3, R3, RD, XA, XM, PV,
           gsem, psem, sa_s, sa_r, sb_s, sb_r, sz_s, sz_r, s3_s, s3_r):
    lat = lax.axis_index("lat")
    lon = lax.axis_index("lon")
    x = lax.rem(lon, 4)
    z = lon // 4
    right = z * 4 + lax.rem(x + 1, 4)
    left = z * 4 + lax.rem(x + 3, 4)
    across = (1 - z) * 4 + x
    south = lat // 16

    barrier = pltpu.get_barrier_semaphore()
    for peer in (right, left, across):
        pl.semaphore_signal(barrier, inc=1, device_id=(lat, peer), device_id_type=MESH)

    def greet(d, carry):
        pl.semaphore_signal(barrier, inc=1, device_id=(lax.rem(lat + d, NLATDEV), lon), device_id_type=MESH)
        return carry

    def grid_copy(n):
        src = n + south * (NB - 1 - 2 * n)
        return pltpu.make_async_copy(
            grid.at[:, pl.ds(pl.multiple_of(src * LB, LB), LB), :], gin.at[n], gsem.at[n])

    def load(n, carry):
        grid_copy(n).start()
        return carry

    lax.fori_loop(0, NB, load, 0)
    lax.fori_loop(1, NLATDEV, greet, 0, unroll=True)
    polys_copy = pltpu.make_async_copy(polys, PV, psem)
    polys_copy.start()

    lane = lax.broadcasted_iota(jnp.int32, (8, 128), 1)
    sub = lax.broadcasted_iota(jnp.int32, (8, 128), 0)
    lane16 = lax.broadcasted_iota(jnp.int32, (16, 128), 1)
    cosl = (lane % 4) < 2
    first = lon * SEG
    base = jnp.where(south == 1, NLATDEV - 1 - lat, lat) * (LB * NB)

    col = lax.broadcasted_iota(jnp.int32, (160, 384), 1)
    slot_of = jnp.where(col < 256, 5 * (col // 8) + (col % 8) // 2, 5 * ((col - 256) // 4) + 4)
    pick_slot = jnp.where(slot_of == lax.broadcasted_iota(jnp.int32, (160, 384), 0), 1.0, 0.0).astype(BF)
    held_pair = jnp.dot(jnp.broadcast_to(prow[...].astype(F32), (8, 160)).astype(BF), pick_slot, preferred_element_type=F32)
    col8 = lax.broadcasted_iota(jnp.int32, (8, 384), 1)
    mrow[...] = M0 + jnp.where(col8 % 2 == 0, held_pair, MW - 1 - held_pair)

    def row(ref, s):
        return jnp.broadcast_to(ref[pl.ds(s, 1), :], (8, 128))

    def seeds(n):
        for g in range(2):
            c = jnp.zeros((8, 128), F32)
            for j in range(8):
                c = jnp.where(sub == j, cnt[base + n * LB + g * 8 + j].astype(F32), c)
            for kt in range(3):
                m = mrow[:, kt * 128:(kt + 1) * 128]
                r1 = fmod(m, c)
                e1 = sincos_turn(r1 / c)
                rp = fmod(r1 * 128.0, c)
                p1 = sincos_turn(rp / c)
                r0 = fmod(rp * (lon * 11 + 5).astype(F32), c)
                w = sincos_turn(r0 / c)
                scale = jnp.where(2.0 * m < c, 1.0 / c, 0.0)
                WC[g, kt] = w[0] * scale
                ws = w[1] * scale
                WS[g, kt] = jnp.where(cosl, ws, -ws) if kt == 2 else ws
                pj = p1
                for j in range(5):
                    if j:
                        pj = cmul(pj, p1)
                    OC[g, kt, j] = pj[0]
                    OS[g, kt, j] = pj[1]
                E = [(jnp.ones((8, 128), F32), jnp.zeros((8, 128), F32)), e1]
                for b in range(2, 16):
                    E.append(cmul(E[b // 2], E[b - b // 2]))
                R2[g, kt] = 2.0 * E[8][0]
                for b in range(16):
                    if kt < 2:
                        SE[g, 2 * kt, b * 8:(b + 1) * 8, :] = E[b][0]
                        SE[g, 2 * kt + 1, b * 8:(b + 1) * 8, :] = E[b][1]
                    else:
                        SE[g, 4, b * 8:(b + 1) * 8, :] = jnp.where(cosl, E[b][0], E[b][1])

    def table(g, s, t, kt):
        r2 = row(R2.at[g, kt], s)
        vs = [SE[g, t, pl.ds(s, 8, stride=8), :], SE[g, t, pl.ds(64 + s, 8, stride=8), :]]
        for _ in range(2, 16):
            vs.append(r2 * vs[-1] - vs[-2])
        return jnp.concatenate(vs, axis=0).astype(BF)

    def one_cycle(n, g, s):
        l = g * 8 + s
        lsrc = l + south * (LB - 1 - 2 * l)
        lim = cnt[base + n * LB + l] - first
        rows = []
        for a in range(11):
            v = gf[a, pl.ds(lsrc, 16, stride=GS), :]
            rows.append(jnp.where(lane16 < lim - 128 * a, v, 0.0).astype(BF))
        lhs = jnp.concatenate(rows, axis=0)
        for kt in range(3):
            if kt < 2:
                tab = jnp.concatenate([table(g, s, 2 * kt, kt), table(g, s, 2 * kt + 1, kt)], axis=1)
            else:
                tab = table(g, s, 4, 2)
            y = jnp.dot(lhs, tab, preferred_element_type=F32)
            wc = row(WC.at[g, kt], s)
            ws = row(WS.at[g, kt], s)
            oc = [row(OC.at[g, kt, j], s) for j in range(5)]
            os = [row(OS.at[g, kt, j], s) for j in range(5)]
            for h in range(2):
                def blk(a, t):
                    return y[a * 16 + h * 8:a * 16 + h * 8 + 8, t * 128:(t + 1) * 128]
                place = pl.ds(h * 8 * GS + l, 8, stride=GS)
                if kt < 2:
                    re = blk(5, 0)
                    im = blk(5, 1)
                    for j in range(1, 6):
                        cp, cm = blk(5 + j, 0), blk(5 - j, 0)
                        sp, sm = blk(5 + j, 1), blk(5 - j, 1)
                        re = re + (oc[j - 1] * (cp + cm) - os[j - 1] * (sp - sm))
                        im = im + (os[j - 1] * (cp - cm) + oc[j - 1] * (sp + sm))
                    ob[2 * kt, place, :] = re * wc - im * ws
                    ob[2 * kt + 1, place, :] = -(im * wc + re * ws)
                else:
                    u = blk(5, 0)
                    v = jnp.zeros_like(u)
                    for j in range(1, 6):
                        p, q = blk(5 + j, 0), blk(5 - j, 0)
                        u = u + oc[j - 1] * (p + q)
                        v = v + os[j - 1] * (p - q)
                    v = jnp.where(cosl, pltpu.roll(v, 126, 1), pltpu.roll(v, 2, 1))
                    w = jnp.where(cosl, u - v, -(u + v))
                    wsw = jnp.where(cosl, pltpu.roll(w, 126, 1), pltpu.roll(w, 2, 1))
                    ob[4, place, :] = w * wc + wsw * ws

    def remote(src, dst, ssem, rsem, la, lo):
        return pltpu.make_async_remote_copy(
            src_ref=src, dst_ref=dst, send_sem=ssem, recv_sem=rsem, device_id=(la, lo), device_id_type=MESH)

    def copy_a(n, side):
        return remote(SB.at[n, 2, side], RA.at[n, side], sa_s, sa_r.at[n, side], lat, (right, left)[side])

    def copy_b(n, side):
        return remote(SB.at[n, 1 + 2 * side], RB.at[n, side], sb_s, sb_r.at[n, side], lat, (right, left)[side])

    def copy_z(n):
        return remote(SZ.at[n], RZ.at[n], sz_s, sz_r.at[n], lat, across)

    LO, HI = (0, 16, 48), (16, 48, 64)

    def copy_3(c, d):
        to = lax.rem(lat + d, NLATDEV)
        return remote(S3.at[to, LO[c]:HI[c], :], R3.at[lat, LO[c]:HI[c], :], s3_s, s3_r.at[c // 2], to, lon)

    def stage_f(n):
        grid_copy(n).wait()

        seeds(n)
        for f in range(16):
            for a in range(11):
                gf[a, f * GS:f * GS + LB, :] = gin[n, f, :, a * 128:(a + 1) * 128].astype(F32)

        def part(g, carry):
            for u in range(UN):
                one_cycle(n, g, u)
            return carry

        for u in range(LB):
            one_cycle(n, u // 8, u % 8)
        for f in range(16):
            h, xd, i = f // 8, (f % 8) // 2, f % 2
            rel = lax.rem(xd + 4 - x, 4)
            for t in range(5):
                v = ob[t, f * GS:f * GS + LB, :]
                SF[n, rel, h, i * LB:(i + 1) * LB, t * 128:(t + 1) * 128] = v
                SB[n, rel, h, i * LB:(i + 1) * LB, t * 128:(t + 1) * 128] = v.astype(BF)

        @pl.when(n == 0)
        def _():
            pl.semaphore_wait(barrier, NLATDEV - 1 + 3)

        for side in range(2):
            copy_a(n, side).start()

    def stage_b(n):
        for side in range(2):
            copy_a(n, side).wait_recv()
            SB[n, 1 + 2 * side, side] = (SF[n, 1 + 2 * side, side] + RA[n, side].astype(F32)).astype(BF)
            copy_b(n, side).start()

    def stage_c(n):
        for side in range(2):
            copy_b(n, side).wait_recv()

        def total(h):
            return SF[n, 0, h] + RB[n, 0, h].astype(F32) + RB[n, 1, h].astype(F32)

        SZ[n] = total(1 - z).astype(BF)
        copy_z(n).start()
        KP[n] = total(z)

    def turn(t):
        return jnp.transpose(TR[t]).reshape(16, 8, 128)

    def send_chunk(c):
        ts = [turn(t) for t in range(5)]
        top = jnp.zeros((8, 128), F32)
        for v in ts:
            top = jnp.maximum(top, jnp.max(jnp.abs(v), axis=0))
        top = jnp.broadcast_to(jnp.max(top, axis=0, keepdims=True), (8, 128))
        code = jnp.ceil(jnp.log2(jnp.maximum(top, 1e-30)) * 64.0)
        inv = STEPS * jnp.exp2(code * (-1.0 / 64.0))
        qs = [jnp.floor(v * inv + 0.5) for v in ts]

        def put(i, r, upper, lower):
            S3[i, r:r + 16, :] = jnp.concatenate([upper, lower], axis=0).astype(jnp.int32).astype(jnp.int16)

        if c == 0:
            MX[...] = qs[4]
            CD[...] = code
        for i in range(NLATDEV):
            half, j = i // 16, i % 16
            re, im = qs[2 * half][j], qs[2 * half + 1][j]
            mix = pltpu.roll(qs[4][i // 2], 4, 0) if i % 2 != c % 2 else qs[4][i // 2]
            if c < 2:
                put(i, LO[c], re, im)
            if c == 1:
                mix0 = pltpu.roll(MX[i // 2], 4, 0) if i % 2 else MX[i // 2]
                put(i, 32, jnp.where(sub < 4, mix0, mix), jnp.where(sub == 0, CD[...], code))
            if c == 2:
                put(i, 48, jnp.where(lane < 64, re, pltpu.roll(mix, 64, 1)), jnp.where(lane < 64, im, pltpu.roll(code, 64, 1)))

        def go(d, carry):
            copy_3(c, d).start()
            return carry

        lax.fori_loop(1, NLATDEV, go, 0, unroll=True)
        R3[lat, LO[c]:HI[c], :] = S3[lat, LO[c]:HI[c], :]

    def stage_d(n):
        copy_z(n).wait_recv()
        width = jnp.where(n < 8, 4 * LB, 2 * LB)
        for i in range(2):
            start = pl.multiple_of(i * width + lax.rem(n, 4) * LB, LB)
            for t in range(5):
                TR[t, pl.ds(start, LB), :] = (
                    KP[n, i * LB:(i + 1) * LB, t * 128:(t + 1) * 128]
                    + RZ[n, i * LB:(i + 1) * LB, t * 128:(t + 1) * 128].astype(F32))
        for c, last in enumerate((3, 7, 9)):
            @pl.when(n == last)
            def _():
                send_chunk(c)

    def step(n, carry):
        @pl.when(n < NB)
        def _():
            stage_f(n)

        @pl.when(n >= 2)
        def _():
            stage_b(n - 2)

        def run(stage, lag):
            def one(k, carry):
                stage(k)
                return carry

            upto = jnp.where(n == NB + 1, NB, jnp.clip(n - lag + 1, 0, NB))
            lax.fori_loop(jnp.clip(n - lag, 0, NB), upto, one, 0)

        run(stage_c, 4)
        run(stage_d, 5)
        return carry

    lax.fori_loop(0, NB + 2, step, 0)

    def drained(ref, sem):
        pltpu.make_async_copy(ref, ref, sem).wait()

    drained(RA, sa_s)
    drained(RB, sb_s)
    drained(SZ, sz_s)
    others = pl.ds(0, NLATDEV - 1)
    drained(S3.at[others], s3_s)
    polys_copy.wait()
    drained(R3.at[others, 0:48, :], s3_r.at[0])

    def roll(v, k):
        return pltpu.roll(v, k % 128, 1) if k % 128 else v

    def scale(v):
        return jnp.exp2(v * (1.0 / 64.0)) * (1.0 / STEPS)

    def take(i, r):
        v = R3[i, r:r + 16, :].astype(jnp.int32).astype(F32)
        return v[:8], v[8:]

    def fold(i, r, sa):
        a = RD[i, r:r + 8, :]
        b = RD[NLATDEV - 1 - i, r:r + 8, :]
        return a + b if sa == 0 else a - b

    def rows_of(sa, f, q):
        return (XA, ((sa * 2 + f) * 2 + q) * 8) if q < 2 else (XM, (sa * 2 + f) * 8)

    def decode_main(i, carry):
        mix, codes = take(i, 32)
        s0 = scale(jnp.broadcast_to(codes[0:1], (8, 128)))
        s1 = scale(jnp.broadcast_to(codes[1:2], (8, 128)))
        for r, sc in ((0, s0), (16, s1)):
            re, im = take(i, r)
            RD[i, r:r + 8, :] = re * sc
            RD[i, r + 8:r + 16, :] = im * sc
        RD[i, 32:40, :] = mix * jnp.where(sub < 4, s0, s1)
        return carry

    def quad_main(qd, carry):
        for sa in range(2):
            for f in range(2):
                for q in range(3):
                    v = []
                    for i in range(4):
                        if q < 2:
                            c0, c1 = fold(qd * 4 + i, q * 8, sa), fold(qd * 4 + i, 16 + q * 8, sa)
                        else:
                            c0 = fold(qd * 4 + i, 32, sa)
                            c1 = pltpu.roll(c0, 4, 0)
                        w = jnp.where(lane < 64, c0, roll(c1, 64)) if f == 0 else jnp.where(lane < 64, roll(c0, 64), c1)
                        v.append(roll(w, 32 * i))
                    ref, r = rows_of(sa, f, q)
                    ref[qd * 5, r:r + 8, :] = v[0]
                    ref[qd * 5 + 1, r:r + 8, :] = v[1]
                    ref[qd * 5 + 2, r:r + 8, :] = jnp.where(lane < 32, v[1], v[2])
                    ref[qd * 5 + 3, r:r + 8, :] = jnp.where(lane < 64, v[2], v[3])
                    ref[qd * 5 + 4, r:r + 8, :] = v[3]
        return carry

    lax.fori_loop(0, NLATDEV, decode_main, 0)
    lax.fori_loop(0, 4, quad_main, 0)

    drained(R3.at[others, 48:64, :], s3_r.at[1])

    def decode_rest(i, carry):
        upper, lower = take(i, 48)
        s2 = scale(jnp.where(lane < 64, pltpu.roll(lower, 64, 1), lower))
        RD[i, 40:48, :] = upper * s2
        RD[i, 48:56, :] = lower * s2
        return carry

    def quad_rest(qd, carry):
        for sa in range(2):
            for i in range(4):
                re, im = fold(qd * 4 + i, 40, sa), fold(qd * 4 + i, 48, sa)
                for f in range(2):
                    for q in range(3):
                        w = roll((re, im, re)[q], 32 * i - 32 * f - (64 if q == 2 else 0))
                        ref, r = rows_of(sa, f, q)
                        ref[qd * 5 + i + 1, r:r + 8, :] = jnp.where(lane // 32 == i, w, ref[qd * 5 + i + 1, r:r + 8, :])
        return carry

    lax.fori_loop(0, NLATDEV, decode_rest, 0)
    lax.fori_loop(0, 4, quad_rest, 0)

    def parts(v):
        hi = v.astype(BF)
        return hi, (v - hi.astype(F32)).astype(BF)

    rr = lax.broadcasted_iota(jnp.int32, (1, ROWS), 1)
    for s in range(5):
        tiles = []
        for t in range(20):
            if s < 4:
                v = jnp.concatenate([XA[t, pl.ds(2 * s + k, 8, stride=8), :] for k in range(2)], axis=0)
            else:
                v = XM[t]
            tiles.append(jnp.concatenate(parts(v), axis=0))
        zz = jnp.concatenate(tiles, axis=1)
        y = lax.dot_general(zz, PV[s], (((1,), (1,)), ((), ())), preferred_element_type=F32)
        half = zz.shape[0] // 2
        y = y[:half] + y[half:]
        sp = MW - pairs[lat * 5 + s]
        in_first = rr < sp
        even = jnp.where(in_first, rr, rr - sp) % 2 == 0

        def pick(k, sa, f, q):
            j = (k * 8 + sa * 4 + f * 2 + q) if s < 4 else ((sa * 2 + f) * 8 + q * 2 + k)
            return y[j:j + 1]

        for f in range(2):
            for q in range(2):
                out[f, s, q:q + 1, :] = jnp.where(
                    even, jnp.where(in_first, pick(0, 0, f, q), pick(1, 0, f, q)),
                    jnp.where(in_first, pick(0, 1, f, q), pick(1, 1, f, q)))


def transform(grid, counts, pairs, polys):
    V = pltpu.VMEM
    dma = pltpu.SemaphoreType.DMA
    return pl.pallas_call(
        kernel,
        in_specs=[
            pl.BlockSpec(memory_space=pltpu.SMEM),
            pl.BlockSpec(memory_space=pltpu.SMEM),
            pl.BlockSpec(memory_space=pltpu.VMEM),
            pl.BlockSpec(memory_space=pl.ANY),
            pl.BlockSpec(memory_space=pl.ANY),
        ],
        out_specs=pl.BlockSpec(memory_space=pltpu.VMEM),
        out_shape=jax.ShapeDtypeStruct((2, 5, 2, ROWS), F32),
        scratch_shapes=[
            V((NB, 16, LB, SEG), BF),
            V((11, 16 * GS, 128), F32),
            V((8, 384), F32),
            V((2, 5, 128, 128), F32),
            V((2, 3, 8, 128), F32),
            V((2, 3, 5, 8, 128), F32),
            V((2, 3, 5, 8, 128), F32),
            V((2, 3, 8, 128), F32),
            V((2, 3, 8, 128), F32),
            V((5, 16 * GS, 128), F32),
            V((NB, 4, 2, 2 * LB, 640), F32),
            V((NB, 4, 2, 2 * LB, 640), BF),
            V((NB, 2, 2 * LB, 640), BF),
            V((NB, 2, 2, 2 * LB, 640), BF),
            V((NB, 2 * LB, 640), F32),
            V((NB, 2 * LB, 640), BF),
            V((NB, 2 * LB, 640), BF),
            V((5, 128, 128), F32),
            V((16, 8, 128), F32),
            V((8, 128), F32),
            V((NLATDEV, 64, 128), jnp.int16),
            V((NLATDEV, 64, 128), jnp.int16),
            V((NLATDEV, 56, 128), F32),
            V((20, 64, 128), F32),
            V((20, 32, 128), F32),
            V((5, ROWS, 2560), BF),
            dma((NB,)), dma(()),
            dma(()), dma((NB, 2)), dma(()), dma((NB, 2)), dma(()), dma((NB,)),
            dma(()), dma((2,)),
        ],
        compiler_params=pltpu.CompilerParams(
            vmem_limit_bytes=56 * 2**20, collective_id=0, has_side_effects=True),
        name="transform",
    )(counts, pairs, pairs[None, :], grid, polys)


def body(grid, cycle_points, pair_slot, polys):
    return jnp.swapaxes(transform(grid, cycle_points, pair_slot, polys), 2, 3)


def solution(mesh):
    in_specs = (P(None, "lat", "lon"), P(), P(), P("lat", None, None))
    out_specs = P("lon", "lat", None, None)
    return jax.shard_map(body, mesh=mesh, in_specs=in_specs, out_specs=out_specs, check_vma=False)
```
